256 devices in a mesh: dp: 8 (over y, core), expert: 32 (over z, x).
Axes of the slice: x: 4, y: 4, z: 8, core: 2. Of those that a mesh axis runs over, the one named last changes fastest.
Arguments:
- tokens: bfloat16 [12288, 2048], P(('dp', 'expert')), may hold values from -6 to 6
- expert_ids: int32 [12288, 8], P(('dp', 'expert')), may hold values from 0 to 31, all different within a row; in each aligned block of 48 rows (0 to 47, 48 to 95, ...) at most 18 rows name the same one
- gate_weights: float32 [12288, 8], P(('dp', 'expert')), may hold values from 0.05 to 1
- up_weight: bfloat16 [32, 2048, 768], P('expert'), may hold values from -0.125 to 0.125
- down_weight: bfloat16 [32, 768, 2048], P('expert'), may hold values from -0.21875 to 0.21875
- out_grad: bfloat16 [12288, 2048], P(('dp', 'expert')), may hold values from -0.59765625 to 0.59765625
Outputs:
- mixed: bfloat16 [12288, 2048], P(('dp', 'expert'))
- grad_tokens: bfloat16 [12288, 2048], P(('dp', 'expert'))
- grad_up: bfloat16 [32, 2048, 768], P('expert')
- grad_down: bfloat16 [32, 768, 2048], P('expert')
The draws below stay inside these ranges and needn't reach their ends.
Inputs may be any that keep to these rules, and one draw needn't show every extreme that they name: `expert_ids`: the 8 experts of a token are distinct. Among the 48 tokens of one device at most 18 name any one expert, and in every draw some device has 18 tokens naming one expert.
All inputs are finite; a program needn't handle non-finite values.
Results may differ from the reference program's by a relative error of at most 0.017.
Values may be sent and summed in bfloat16 or wider, within the bound.
A program may use at most 128 MiB of HBM per device.

```python
import math
import jax
import jax.numpy as jnp
import numpy as np
from jax import lax

D = 2048
FF = 768
TOK_DEV = 48
TOP = 8
SLOT = 18
EXPERTS = 32
GROUP_TOKENS = 1536
TOKENS = 12288
N_DP = 8
N_EXPERT = 32


def shard_levels(own_key, dims, shards, least, largest):
    def one(position, blocks):
        steps = jax.random.uniform(jax.random.fold_in(jax.random.fold_in(own_key, 6), position), (blocks,), jnp.float32, least / len(shards), largest / len(shards))
        return jnp.repeat(jnp.exp(steps), dims[position] // blocks).reshape((-1,) + (1,) * (len(dims) - position - 1))

    gain = one(*shards[0])
    for cut in shards[1:]:
        gain = gain * one(*cut)
    return gain


def assign_block(stream_key, own, number, rows, count, top, reach, skew):
    order = jax.random.permutation(stream_key, count)
    heavy_load, common = portions_of(count, rows * top, reach, skew, True), portions_of(count, rows * top, reach, skew, False)
    places = jnp.arange(count)

    def named(lengths, offset_by):
        used = int((lengths > 0).sum())
        fixed = max(1, used // 4)
        passed = fixed + (places - fixed + offset_by * (used - fixed)) % max(1, count - fixed)
        return jnp.zeros((count,), jnp.int32).at[order[jnp.where(places < fixed, places, passed)]].set(jnp.asarray(lengths, jnp.int32))

    lengths = jnp.where(number % 4 == 0, named(heavy_load, number // 4), named(common, number - number // 4 - 1))
    mixed = jax.random.permutation(jax.random.fold_in(own, 3), count)
    source_of, taker = mixed[0:count // 2 * 2:2], mixed[1:count // 2 * 2:2]
    room = jnp.minimum(lengths[source_of] - 1, reach - lengths[taker]) // 2
    room = jnp.where((source_of == order[0]) | (taker == order[0]) | (lengths[taker] == 0), 0, jnp.maximum(room, 0))
    passed = jax.random.randint(jax.random.fold_in(own, 4), (count // 2,), 0, 1 << 20) % (room + 1)
    lengths = lengths.at[source_of].add(-passed).at[taker].add(passed)
    members = jnp.searchsorted(jnp.cumsum(lengths), jnp.arange(rows * top), side="right").astype(jnp.int32)
    table = members.reshape(top, rows).T
    table = table[jax.random.permutation(jax.random.fold_in(own, 1), rows)]
    offset_by = jax.random.randint(jax.random.fold_in(own, 2), (rows, 1), 0, top)
    return jnp.take_along_axis(table, (jnp.arange(top)[None, :] + offset_by) % top, axis=1)


def portions_of(number_of, total, most, lean, full):
    weights = [(1 << 20) // math.isqrt(rank ** lean) + 1 for rank in range(1, number_of + 1)]
    largest = most if full else min(most, max(-(-total // number_of), total * weights[0] // sum(weights)))
    least = 1 if total - largest >= number_of - 1 else 0
    holding, spare = [largest] + [least] * (number_of - 1), total - largest - least * (number_of - 1)
    while spare > 0:
        candidates = [i for i in range(1, number_of) if holding[i] < largest] or [i for i in range(1, number_of) if holding[i] < most]
        pool, remaining = sum([weights[i] for i in candidates]), spare
        for i in candidates:
            addition = min(most - holding[i], max(1, remaining * weights[i] // pool), spare)
            holding[i] = holding[i] + addition
            spare = spare - addition
    return np.array(holding)


def centred(stream_key, extent, scale, limit, shards=(), held_as=jnp.bfloat16):
    result = scale * jax.random.normal(stream_key, extent, jnp.float32)
    if shards:
        result = result * shard_levels(stream_key, extent, shards, -0.22, 0.18)
    return jnp.clip(result, -limit, limit).astype(held_as)


def setup_inputs(seed: int = 0) -> dict:
    arg_keys = jax.random.split(jax.random.key(seed), 7)
    tokens = centred(arg_keys[0], (TOKENS, D), 1.0, 6.0, ((0, 256),))
    expert_ids_keys = jax.random.split(jax.random.fold_in(arg_keys[1], 1), TOKENS // TOK_DEV)
    expert_ids_turns = jax.random.permutation(jax.random.fold_in(arg_keys[1], 3), TOKENS // TOK_DEV)
    expert_ids = jax.vmap(lambda own, number: assign_block(jax.random.fold_in(arg_keys[1], 2), own, number, TOK_DEV, EXPERTS, TOP, SLOT, 2))(expert_ids_keys, expert_ids_turns).reshape((TOKENS, TOP))
    gate_weights = jnp.clip(jnp.exp(math.log(1.0) - 2.9957323 * jax.random.uniform(arg_keys[2], (TOKENS, TOP), jnp.float32) ** shard_levels(arg_keys[2], (TOKENS, TOP), ((0, 256),), -0.2, 0.2)), 0.05, 1.0)
    up_weight = centred(arg_keys[3], (EXPERTS, D, FF), D ** -0.5, 0.125, ((0, 32),))
    down_weight = centred(arg_keys[4], (EXPERTS, FF, D), FF ** -0.5, 0.21875, ((0, 32),))
    out_grad = centred(arg_keys[5], (TOKENS, D), 0.1, 0.59765625, ((0, 256),))
    return {"tokens": tokens, "expert_ids": expert_ids, "gate_weights": gate_weights, "up_weight": up_weight, "down_weight": down_weight, "out_grad": out_grad}


def silu_slope(pre_act):
    sigmoid = jax.nn.sigmoid(pre_act)
    return sigmoid * (1.0 + pre_act * (1.0 - sigmoid))


def reference(tokens, expert_ids, gate_weights, up_weight, down_weight, out_grad):
    capacity = N_EXPERT * SLOT
    assigned = GROUP_TOKENS * TOP
    up_total = jnp.zeros((EXPERTS, D, FF), jnp.float32)
    down_total = jnp.zeros((EXPERTS, FF, D), jnp.float32)
    mixed_parts = []
    grad_parts = []
    for group in range(N_DP):
        low = group * GROUP_TOKENS
        group_tokens = tokens[low:low + GROUP_TOKENS]
        flat_ids = expert_ids[low:low + GROUP_TOKENS].reshape(-1)
        group_gates = gate_weights[low:low + GROUP_TOKENS]
        owner = (jnp.arange(assigned, dtype=jnp.int32) // TOP).astype(jnp.int32)
        scaled = (group_gates.reshape(-1)[:, None] * out_grad[low:low + GROUP_TOKENS][owner].astype(jnp.float32)).astype(jnp.bfloat16)

        def one_expert(expert):
            misses = (flat_ids != expert).astype(jnp.int32)
            picked = jnp.argsort(misses, stable=True)[:capacity].astype(jnp.int32)
            present = misses[picked] == 0
            rows_x = jnp.where(present[:, None], group_tokens[picked // TOP], jnp.zeros((), jnp.bfloat16))
            rows_dy = jnp.where(present[:, None], scaled[picked], jnp.zeros((), jnp.bfloat16))
            up_local = up_weight[expert]
            down_local = down_weight[expert]
            pre_act = jnp.dot(rows_x, up_local, preferred_element_type=jnp.float32)
            hidden = jax.nn.silu(pre_act).astype(jnp.bfloat16)
            expert_out = jnp.dot(hidden, down_local, preferred_element_type=jnp.float32).astype(jnp.bfloat16)
            linear = jnp.dot(rows_dy, down_local.T, preferred_element_type=jnp.float32)
            pre_grad = (linear * silu_slope(pre_act)).astype(jnp.bfloat16)
            grad_rows = jnp.dot(pre_grad, up_local.T, preferred_element_type=jnp.float32).astype(jnp.bfloat16)
            up_part = jnp.dot(rows_x.T, pre_grad, preferred_element_type=jnp.float32).astype(jnp.bfloat16)
            down_part = jnp.dot(hidden.T, rows_dy, preferred_element_type=jnp.float32).astype(jnp.bfloat16)
            slots = jnp.where(present, picked, assigned).astype(jnp.int32)
            return expert_out, grad_rows, slots, up_part, down_part

        outs_all, grads_all, slots_all, up_parts, down_parts = lax.map(one_expert, jnp.arange(EXPERTS, dtype=jnp.int32))
        slot_list = slots_all.reshape(-1)
        flat_out = jnp.zeros((assigned + 1, D), jnp.bfloat16).at[slot_list].set(outs_all.reshape(-1, D))
        flat_grad = jnp.zeros((assigned + 1, D), jnp.bfloat16).at[slot_list].set(grads_all.reshape(-1, D))
        per_pair = flat_out[:assigned].reshape(GROUP_TOKENS, TOP, D).astype(jnp.float32)
        mixed_parts.append(jnp.sum(group_gates[:, :, None] * per_pair, axis=1).astype(jnp.bfloat16))
        grad_pairs = flat_grad[:assigned].reshape(GROUP_TOKENS, TOP, D).astype(jnp.float32)
        grad_parts.append(jnp.sum(grad_pairs, axis=1).astype(jnp.bfloat16))
        up_total = up_total + up_parts.astype(jnp.float32)
        down_total = down_total + down_parts.astype(jnp.float32)
    mixed = jnp.concatenate(mixed_parts, axis=0)
    grad_tokens = jnp.concatenate(grad_parts, axis=0)
    return mixed, grad_tokens, up_total.astype(jnp.bfloat16), down_total.astype(jnp.bfloat16)
```

```python
import functools

import jax
import jax.numpy as jnp
from jax import lax
from jax.experimental import pallas as pl
from jax.experimental.pallas import tpu as pltpu
from jax.sharding import PartitionSpec as P

BF16 = jnp.bfloat16
F32 = jnp.float32
MESH_ID = pl.DeviceIdType.MESH


def mm(left, right, left_dim=1, right_dim=0):
    return lax.dot_general(
        left, right, (((left_dim,), (right_dim,)), ((), ())), preferred_element_type=F32
    )


class Cfg:
    def __init__(self, nz, nx, ny, tok, top, width, hidden, nc):
        self.nz, self.nx, self.ny = nz, nx, ny
        self.tok, self.top, self.width, self.hidden, self.nc = tok, top, width, hidden, nc
        self.experts = nz * nx
        self.slot = tok * top * 3 // (2 * self.experts)
        self.rows_x = nz * self.slot
        self.rows = nx * self.rows_x
        self.seen = nz * tok
        self.cw = width // nc


def kernel(cfg, *refs):
    nz, nx, ny, tok, nc, cw = cfg.nz, cfg.nx, cfg.ny, cfg.tok, cfg.nc, cfg.cw
    rx, rows, seen, experts = cfg.rows_x, cfg.rows, cfg.seen, cfg.experts
    width, hid_w = cfg.width, cfg.hidden
    (tok_ref, og_ref, ids_ref, gate_ref, up_hbm, down_hbm, mixed_ref, gtok_ref, gup_ref, gdown_ref) = refs[:10]
    (zbuf, zmeta, xsend, xrecv, upv, downv, pre, lin, hid, pgr, onehot, onehot_t, gates,
     csend, crecv, pbuf, rsbuf, fin, g_down, g_up, c_down, c_up, r_down, r_up, f_down, f_up,
     w_sem, z_ss, z_rs, x_ss, x_rs, c_ss, c_rs, s_ss, s_rs, y_ss, y_rs, l_sem) = refs[10:]

    dp = lax.axis_index("dp")
    ex = lax.axis_index("expert")
    y, core = dp // 2, lax.rem(dp, 2)
    z, x = ex // nx, lax.rem(ex, nx)

    def at_z(step):
        return (dp, lax.rem(z + step + nz, nz) * nx + x)

    def at_x(step):
        return (dp, z * nx + lax.rem(x + step + nx, nx))

    def at_y(step):
        return (lax.rem(y + step + ny, ny) * 2 + core, ex)

    other_core = (y * 2 + 1 - core, ex)

    def copy(src, dst, ss, rs, to):
        return pltpu.make_async_remote_copy(
            src_ref=src, dst_ref=dst, send_sem=ss, recv_sem=rs, device_id=to, device_id_type=MESH_ID
        )

    w_up = pltpu.make_async_copy(up_hbm.at[0], upv, w_sem.at[0])
    w_down = pltpu.make_async_copy(down_hbm.at[0], downv, w_sem.at[1])
    w_up.start()
    w_down.start()

    partners = [at_z(1), at_z(-1)] + [at_x(j) for j in range(1, nx)]
    if ny > 1:
        partners += [at_y(1), at_y(-1), other_core]
    barrier = pltpu.get_barrier_semaphore()
    for partner in partners:
        pl.semaphore_signal(barrier, inc=1, device_id=partner, device_id_type=MESH_ID)

    for k in range(nc):
        zbuf[k, 0:tok, :] = tok_ref[:, k * cw:(k + 1) * cw]
        zbuf[nc + k, 0:tok, :] = og_ref[:, k * cw:(k + 1) * cw]
    lane = lax.broadcasted_iota(jnp.int32, (tok, 128), 1)
    lane_e = lane & (experts - 1)
    hit = jnp.zeros((tok, 128), F32)
    gate = jnp.zeros((tok, 128), F32)
    for k in range(cfg.top):
        match = ids_ref[:, k:k + 1] == lane_e
        hit = hit + jnp.where(match, 1.0, 0.0)
        gate = gate + jnp.where(match, gate_ref[:, k:k + 1], 0.0)
    row_t = lax.broadcasted_iota(jnp.int32, (tok, tok), 0)
    col_t = lax.broadcasted_iota(jnp.int32, (tok, tok), 1)
    earlier = jnp.where(col_t < row_t, 1.0, 0.0).astype(BF16)
    before = mm(earlier, hit.astype(BF16))
    place = jnp.where(hit > 0.5, before, -1.0)
    high = gate.astype(BF16).astype(F32)
    rest = gate - high
    middle = rest.astype(BF16).astype(F32)
    low = rest - middle
    table = jnp.where(
        lane < experts, place,
        jnp.where(lane < 2 * experts, high,
                  jnp.where(lane < 3 * experts, middle,
                            jnp.where(lane < 4 * experts, low, 0.0))))
    zmeta[0:tok, :] = table.astype(BF16)

    pl.semaphore_wait(barrier, len(partners))

    def ways(k):
        plus = nz // 2 if k % 2 == 0 else (nz - 1) // 2
        return plus, nz - 1 - plus

    def z_copy(k, way, hop):
        source = hop - 1 if way == 0 else (nz - hop + 1) % nz
        target = hop if way == 0 else nz - hop
        buf = zmeta if k == 2 * nc else zbuf.at[k]
        return copy(
            buf.at[pl.ds(source * tok, tok)], buf.at[pl.ds(target * tok, tok)],
            z_ss.at[k, target - 1], z_rs.at[k, target - 1], at_z(1 if way == 0 else -1))

    def z_step(k, hop):
        for way in (0, 1):
            if 1 <= hop <= ways(k)[way]:
                z_copy(k, way, hop).wait_recv()
            if hop + 1 <= ways(k)[way]:
                z_copy(k, way, hop + 1).start()

    def build_tables():
        meta = zmeta[...].astype(F32)
        lanes = lax.broadcasted_iota(jnp.int32, (seen, 128), 1)
        row = lax.broadcasted_iota(jnp.int32, (seen, 1), 0)
        source = jnp.zeros((seen, 1), F32)
        for q in range(1, nz):
            source = source + jnp.where(row >= q * tok, 1.0, 0.0)
        wide = -(-rows // 128) * 128
        place_lane = lax.broadcasted_iota(jnp.int32, (seen, wide), 1)
        hot = jnp.zeros((seen, wide), F32)
        for j in range(nx):
            expert = z * nx + lax.rem(x + j, nx)
            spot = jnp.sum(jnp.where(lanes == expert, meta, 0.0), axis=1, keepdims=True)
            value = jnp.where(spot > -0.5, spot + cfg.slot * source + rx * j, -1.0).astype(jnp.int32)
            hot = hot + jnp.where(place_lane == value, 1.0, 0.0)
        onehot_t[...] = hot[:, 0:rows].astype(BF16)
        onehot[...] = hot.T[0:rows].astype(BF16)
        picked = mm(onehot[...], zmeta[...])
        lanes_r = lax.broadcasted_iota(jnp.int32, (rx, 128), 1)
        for j in range(nx):
            expert = z * nx + lax.rem(x + j, nx)
            mine = ((lanes_r & (experts - 1)) == expert) & (lanes_r >= experts)
            value = jnp.sum(jnp.where(mine, picked[j * rx:(j + 1) * rx], 0.0), axis=1, keepdims=True)
            gates[j * rx:(j + 1) * rx, :] = jnp.broadcast_to(value, (rx, 128))

    def x_copy(k, j):
        return copy(
            xsend.at[k, pl.ds((j - 1) * rx, rx)], xrecv.at[k, pl.ds(j * rx, rx)],
            x_ss.at[k, j - 1], x_rs.at[k, j - 1], at_x(j))

    def dispatch(k):
        packed = mm(onehot[...], zbuf[k])
        if k >= nc:
            packed = packed * gates[:, 0:1]
        packed = packed.astype(BF16)
        xsend[k] = packed[rx:]
        xrecv[k, 0:rx, :] = packed[0:rx]
        for j in range(1, nx):
            x_copy(k, j).start()

    def arrive(k):
        for j in range(1, nx):
            x_copy(k, j).wait_recv()
        if k < nc:
            if k == 0:
                w_up.wait()
            part = mm(xrecv[k], upv[k * cw:(k + 1) * cw, :])
            if k == 0:
                pre[...] = part
            else:
                pre[...] += part
        else:
            c = k - nc
            if c == 0:
                w_down.wait()
            part = mm(xrecv[k], downv[:, c * cw:(c + 1) * cw], 1, 1)
            if c == 0:
                lin[...] = part
            else:
                lin[...] += part
            g_down[:, c * cw:(c + 1) * cw] = mm(hid[...], xrecv[k], 0, 0).astype(BF16)

    blk = 16

    def make_hidden():
        def body(i, carry):
            at = pl.ds(pl.multiple_of(i * blk, blk), blk)
            p = pre[at, :]
            hid[at, :] = (p * jax.nn.sigmoid(p)).astype(BF16)
            return carry
        lax.fori_loop(0, rows // blk, body, 0)

    def make_pre_grad():
        def body(i, carry):
            at = pl.ds(pl.multiple_of(i * blk, blk), blk)
            p = pre[at, :]
            s = jax.nn.sigmoid(p)
            pgr[at, :] = (lin[at, :] * (s * (1.0 + p * (1.0 - s)))).astype(BF16)
            return carry
        lax.fori_loop(0, rows // blk, body, 0)

    def c_copy(m, j):
        return copy(
            csend.at[m, pl.ds((j - 1) * rx, rx)], crecv.at[m, pl.ds(j * rx, rx)],
            c_ss.at[m, j - 1], c_rs.at[m, j - 1], at_x(-j))

    def send_back(m):
        c = m % nc
        if m < nc:
            out = mm(hid[...], downv[:, c * cw:(c + 1) * cw])
        else:
            out = mm(pgr[...], upv[c * cw:(c + 1) * cw, :], 1, 1)
        out = out.astype(BF16)
        csend[m] = out[rx:]
        crecv[m, 0:rx, :] = out[0:rx]
        for j in range(1, nx):
            c_copy(m, j).start()

    def s_copy(m, way, hop):
        plus, minus = ways(m)
        slot = plus - hop + 1 if way == 0 else nz - (minus - hop + 1)
        at = hop - 1 if way == 0 else plus + hop - 1
        return copy(
            pbuf.at[m, pl.ds(slot * tok, tok)], rsbuf.at[m, at],
            s_ss.at[m, at], s_rs.at[m, at], at_z(-1 if way == 0 else 1))

    def s_step(m, hop):
        for way in (0, 1):
            count = ways(m)[way]
            if 1 <= hop <= count:
                s_copy(m, way, hop).wait_recv()
                at = hop - 1 if way == 0 else ways(m)[0] + hop - 1
                got = rsbuf[m, at].astype(F32)
                left = count - hop
                if left == 0:
                    fin[m] += got
                else:
                    slot = left if way == 0 else nz - left
                    sl = slice(slot * tok, (slot + 1) * tok)
                    pbuf[m, sl, :] = (pbuf[m, sl, :].astype(F32) + got).astype(BF16)
            if hop + 1 <= count:
                s_copy(m, way, hop + 1).start()
        if hop == max(ways(m)):
            c = m % nc
            target = mixed_ref if m < nc else gtok_ref
            target[:, c * cw:(c + 1) * cw] = fin[m].astype(BF16)

    def combine(m):
        for j in range(1, nx):
            c_copy(m, j).wait_recv()
        got = crecv[m]
        if m < nc:
            got = (got.astype(F32) * gates[:, 0:1]).astype(BF16)
        part = mm(onehot_t[...], got)
        fin[m] = part[0:tok]
        pbuf[m, tok:, :] = part[tok:].astype(BF16)
        s_step(m, 0)

    mats = [(g_down, c_down, r_down, f_down, gdown_ref), (g_up, c_up, r_up, f_up, gup_ref)]

    def y_copies(w):
        g, cr, r, f, out = mats[w]
        half = g.shape[0] // 2
        shard = half // 4
        part = shard // 2

        def of(step, b=0):
            return pl.multiple_of(lax.rem(y + step + ny, ny) * shard + b * part, part)

        def final(step, b, count):
            return out.at[0, pl.ds(pl.multiple_of(core * half + of(step, b), part), count)]

        def sem(i):
            return y_ss.at[w, i], y_rs.at[w, i]

        return dict(
            core=lambda: copy(g.at[pl.ds(pl.multiple_of((1 - core) * half, half), half)], cr, *sem(0), other_core),
            far_a=lambda: copy(cr.at[pl.ds(of(2, 0), part)], r.at[0], *sem(1), at_y(1)),
            far_b=lambda: copy(cr.at[pl.ds(of(2, 1), part)], r.at[1], *sem(2), at_y(-1)),
            near_b=lambda: copy(cr.at[pl.ds(of(1, 1), part)], r.at[2], *sem(3), at_y(1)),
            near_a=lambda: copy(cr.at[pl.ds(of(-1, 0), part)], r.at[3], *sem(4), at_y(-1)),
            two_a=lambda: copy(r.at[0], r.at[4], *sem(5), at_y(1)),
            two_b=lambda: copy(r.at[1], r.at[5], *sem(6), at_y(-1)),
            out_p=lambda: copy(f, final(0, 0, shard), *sem(7), at_y(1)),
            out_m=lambda: copy(f, final(0, 0, shard), *sem(8), at_y(-1)),
            out_c=lambda: copy(f, final(0, 0, shard), *sem(9), other_core),
            fwd_a=lambda: copy(final(-1, 0, part), final(-1, 0, part), *sem(10), at_y(1)),
            fwd_b=lambda: copy(final(1, 1, part), final(1, 1, part), *sem(11), at_y(-1)),
            cor_p=lambda: copy(final(-1, 0, shard), final(-1, 0, shard), *sem(12), other_core),
            cor_m=lambda: copy(final(1, 0, shard), final(1, 0, shard), *sem(13), other_core),
            cor_f=lambda: copy(final(2, 0, shard), final(2, 0, shard), *sem(14), other_core),
            own=lambda: pltpu.make_async_copy(f, final(0, 0, shard), l_sem.at[w]),
        )

    def add_rows(target, t0, source, s0, count, extra=None):
        size = 16 if count % 16 == 0 else count

        def body(i, carry):
            a = pl.ds(pl.multiple_of(t0 + i * size, size), size)
            b = pl.ds(pl.multiple_of(s0 + i * size, size), size)
            target[a, :] = (target[a, :].astype(F32) + source[b, :].astype(F32)).astype(BF16)
            return carry
        lax.fori_loop(0, count // size, body, 0)

    def y_step(w, step):
        g, cr, r, f, out = mats[w]
        half = g.shape[0] // 2
        shard = half // 4
        part = shard // 2
        cp = y_copies(w)

        def of(move, b=0):
            return pl.multiple_of(lax.rem(y + move + ny, ny) * shard + b * part, part)

        if step == 1:
            cp["core"]().start()
        elif step == 2:
            cp["core"]().wait_recv()
            add_rows(cr, 0, g, pl.multiple_of(core * half, half), half)
            for name in ("far_a", "far_b", "near_b", "near_a"):
                cp[name]().start()
        elif step == 3:
            cp["far_a"]().wait_recv()
            add_rows(r.at[0], 0, cr, of(1, 0), part)
            cp["two_a"]().start()
            cp["far_b"]().wait_recv()
            add_rows(r.at[1], 0, cr, of(-1, 1), part)
            cp["two_b"]().start()
        elif step == 4:
            for name in ("near_a", "near_b", "two_a", "two_b"):
                cp[name]().wait_recv()
            size = 16 if part % 16 == 0 else part
            for b, near, two in ((0, 3, 4), (1, 2, 5)):
                def body(i, carry):
                    a = pl.ds(pl.multiple_of(i * size, size), size)
                    c = pl.ds(pl.multiple_of(of(0, b) + i * size, size), size)
                    total = cr[c, :].astype(F32) + r[near, a, :].astype(F32) + r[two, a, :].astype(F32)
                    f[pl.ds(pl.multiple_of(b * part + i * size, size), size), :] = total.astype(BF16)
                    return carry
                lax.fori_loop(0, part // size, body, 0)
            for name in ("out_p", "out_m", "out_c", "own"):
                cp[name]().start()
        elif step == 5:
            cp["out_p"]().wait_recv()
            cp["fwd_a"]().start()
            cp["cor_p"]().start()
            cp["out_m"]().wait_recv()
            cp["fwd_b"]().start()
            cp["cor_m"]().start()
        elif step == 6:
            cp["fwd_a"]().wait_recv()
            cp["fwd_b"]().wait_recv()
            cp["cor_f"]().start()
        elif step == 7:
            for name in ("out_c", "cor_p", "cor_m", "cor_f"):
                cp[name]().wait_recv()
            cp["own"]().wait()

    hops = nz // 2
    events = []
    for h in range(hops + 1):
        events.append((h - 0.5, 2 * nc, h))
    for k in range(2 * nc):
        for h in range(hops + 1):
            events.append((h if k == 0 else 2 * k + h + 1, k, h))
    events.sort()
    last_x = -1
    for _, k, h in events:
        z_step(k, h)
        if h == hops:
            if k == 2 * nc:
                build_tables()
            else:
                dispatch(k)
                if k >= 2 and k - 2 < nc + 1:
                    arrive(k - 2)
                    last_x = k - 2
                    if last_x == nc - 1:
                        make_hidden()
    back = 0
    for k in range(last_x + 1, 2 * nc):
        arrive(k)
        if k == nc - 1:
            make_hidden()
        if k >= 2 * nc - 2:
            send_back(back)
            back += 1
    do_y = ny > 1
    if do_y:
        y_step(0, 1)
    make_pre_grad()
    for c in range(nc):
        g_up[c * cw:(c + 1) * cw, :] = mm(xrecv[c], pgr[...], 0, 0).astype(BF16)
    if do_y:
        y_step(1, 1)
        y_step(0, 2)
    ys = [(0, 3), (1, 2), (0, 4), (1, 3), (0, 5), (1, 4), (0, 6), (1, 5), (0, 7), (1, 6), (1, 7)]
    if not do_y:
        ys = []
    s_events = []
    for m in range(2 * nc):
        if back < 2 * nc:
            send_back(back)
            back += 1
        combine(m)
        if ys:
            y_step(*ys.pop(0))
        if m >= 1:
            s_step(m - 1, 1)
            s_step(m - 1, 2)
        if m >= 2:
            for h in range(3, hops + 1):
                s_step(m - 2, h)
    last = 2 * nc - 1
    for h in range(3, hops + 1):
        s_step(last - 1, h)
    if ys:
        y_step(*ys.pop(0))
    for h in range(1, hops + 1):
        s_step(last, h)
        if ys:
            y_step(*ys.pop(0))
    while ys:
        y_step(*ys.pop(0))

    for k in range(2 * nc + 1):
        for way in (0, 1):
            for h in range(1, ways(k)[way] + 1):
                z_copy(k, way, h).wait_send()
    for k in range(2 * nc):
        for j in range(1, nx):
            x_copy(k, j).wait_send()
            c_copy(k, j).wait_send()
        for way in (0, 1):
            for h in range(1, ways(k)[way] + 1):
                s_copy(k, way, h).wait_send()
    if do_y:
        for w in (0, 1):
            for name, cp in y_copies(w).items():
                if name != "own":
                    cp().wait_send()


def run(cfg, tokens, expert_ids, gate_weights, up_weight, down_weight, out_grad):
    tok, width, hid_w, nc, cw = cfg.tok, cfg.width, cfg.hidden, cfg.nc, cfg.cw
    rows, rx, seen, nz, nx = cfg.rows, cfg.rows_x, cfg.seen, cfg.nz, cfg.nx
    vmem = pl.BlockSpec(memory_space=pltpu.VMEM)
    anywhere = pl.BlockSpec(memory_space=pl.ANY)
    dma = pltpu.SemaphoreType.DMA
    scratch = [
        pltpu.VMEM((2 * nc, seen, cw), BF16),
        pltpu.VMEM((seen, 128), BF16),
        pltpu.VMEM((2 * nc, rows - rx, cw), BF16),
        pltpu.VMEM((2 * nc, rows, cw), BF16),
        pltpu.VMEM((width, hid_w), BF16),
        pltpu.VMEM((hid_w, width), BF16),
        pltpu.VMEM((rows, hid_w), F32),
        pltpu.VMEM((rows, hid_w), F32),
        pltpu.VMEM((rows, hid_w), BF16),
        pltpu.VMEM((rows, hid_w), BF16),
        pltpu.VMEM((rows, seen), BF16),
        pltpu.VMEM((seen, rows), BF16),
        pltpu.VMEM((rows, 128), F32),
        pltpu.VMEM((2 * nc, rows - rx, cw), BF16),
        pltpu.VMEM((2 * nc, rows, cw), BF16),
        pltpu.VMEM((2 * nc, seen, cw), BF16),
        pltpu.VMEM((2 * nc, nz - 1, tok, cw), BF16),
        pltpu.VMEM((2 * nc, tok, cw), F32),
        pltpu.VMEM((hid_w, width), BF16),
        pltpu.VMEM((width, hid_w), BF16),
        pltpu.VMEM((hid_w // 2, width), BF16),
        pltpu.VMEM((width // 2, hid_w), BF16),
        pltpu.VMEM((6, hid_w // 16, width), BF16),
        pltpu.VMEM((6, width // 16, hid_w), BF16),
        pltpu.VMEM((hid_w // 8, width), BF16),
        pltpu.VMEM((width // 8, hid_w), BF16),
        dma((2,)),
        dma((2 * nc + 1, nz - 1)),
        dma((2 * nc + 1, nz - 1)),
        dma((2 * nc, nx - 1)),
        dma((2 * nc, nx - 1)),
        dma((2 * nc, nx - 1)),
        dma((2 * nc, nx - 1)),
        dma((2 * nc, nz - 1)),
        dma((2 * nc, nz - 1)),
        dma((2, 15)),
        dma((2, 15)),
        dma((2,)),
    ]
    return pl.pallas_call(
        functools.partial(kernel, cfg),
        out_shape=(
            jax.ShapeDtypeStruct((tok, width), BF16),
            jax.ShapeDtypeStruct((tok, width), BF16),
            jax.ShapeDtypeStruct((1, width, hid_w), BF16),
            jax.ShapeDtypeStruct((1, hid_w, width), BF16),
        ),
        in_specs=[vmem, vmem, vmem, vmem, anywhere, anywhere],
        out_specs=(vmem, vmem, anywhere, anywhere),
        scratch_shapes=scratch,
        compiler_params=pltpu.CompilerParams(
            collective_id=0, has_side_effects=True, vmem_limit_bytes=60 * 2**20
        ),
        name="expert_layer",
    )(tokens, out_grad, expert_ids, gate_weights, up_weight, down_weight)


def solution(mesh):
    dp, experts = mesh.shape["dp"], mesh.shape["expert"]

    def shards(tokens, expert_ids, gate_weights, up_weight, down_weight, out_grad):
        cfg = Cfg(8, experts // 8, dp // 2, tokens.shape[0], expert_ids.shape[1], tokens.shape[1],
                  up_weight.shape[2], 4)
        return run(cfg, tokens, expert_ids, gate_weights, up_weight, down_weight, out_grad)

    return jax.shard_map(
        shards,
        mesh=mesh,
        in_specs=(
            P(("dp", "expert"), None),
            P(("dp", "expert"), None),
            P(("dp", "expert"), None),
            P("expert", None, None),
            P("expert", None, None),
            P(("dp", "expert"), None),
        ),
        out_specs=(
            P(("dp", "expert"), None),
            P(("dp", "expert"), None),
            P("expert", None, None),
            P("expert", None, None),
        ),
        check_vma=False,
    )
```

```python
import functools

import jax
import jax.numpy as jnp
from jax import lax
from jax.experimental import pallas as pl
from jax.experimental.pallas import tpu as pltpu
from jax.sharding import PartitionSpec as P

BF16 = jnp.bfloat16
F32 = jnp.float32
MESH_ID = pl.DeviceIdType.MESH
LAG = 2


def mm(left, right, left_dim=1, right_dim=0):
    return lax.dot_general(
        left, right, (((left_dim,), (right_dim,)), ((), ())), preferred_element_type=F32
    )


class Cfg:
    def __init__(self, nz, nx, ny, tok, top, width, hidden, nc):
        self.nz, self.nx, self.ny = nz, nx, ny
        self.tok, self.top, self.width, self.hidden, self.nc = tok, top, width, hidden, nc
        self.experts = nz * nx
        self.slot = tok * top * 3 // (2 * self.experts)
        self.rows_x = nz * self.slot
        self.rows = nx * self.rows_x
        self.seen = nz * tok
        self.cw = width // nc


def kernel(cfg, *refs):
    nz, nx, ny, tok, nc, cw = cfg.nz, cfg.nx, cfg.ny, cfg.tok, cfg.nc, cfg.cw
    rx, rows, seen, experts = cfg.rows_x, cfg.rows, cfg.seen, cfg.experts
    width, hid_w = cfg.width, cfg.hidden
    (tok_ref, og_ref, ids_ref, gate_ref, up_hbm, down_hbm, mixed_ref, gtok_ref, gup_ref, gdown_ref) = refs[:10]
    (zbuf, zmeta, xsend, xrecv, upv, downv, pre, lin, hid, pgr, onehot, onehot_t, gates,
     csend, crecv, pbuf, rsbuf, fin, g_down, g_up, c_down, c_up, r_down, r_up, f_down, f_up,
     w_sem, z_ss, z_rs, x_ss, x_rs, c_ss, c_rs, s_ss, s_rs, y_ss, y_rs, l_sem) = refs[10:]

    dp = lax.axis_index("dp")
    ex = lax.axis_index("expert")
    y, core = dp // 2, lax.rem(dp, 2)
    z, x = ex // nx, lax.rem(ex, nx)

    def at_z(step):
        return (dp, lax.rem(z + step + nz, nz) * nx + x)

    def at_x(step):
        return (dp, z * nx + lax.rem(x + step + nx, nx))

    def at_y(step):
        return (lax.rem(y + step + ny, ny) * 2 + core, ex)

    other_core = (y * 2 + 1 - core, ex)

    def copy(src, dst, ss, rs, to):
        return pltpu.make_async_remote_copy(
            src_ref=src, dst_ref=dst, send_sem=ss, recv_sem=rs, device_id=to, device_id_type=MESH_ID
        )

    own_block = []
    for k in range(2 * nc):
        c = k % nc
        source = tok_ref if k < nc else og_ref
        own_block.append(pltpu.make_async_copy(
            source.at[:, pl.ds(c * cw, cw)], zbuf.at[k, pl.ds(0, tok)], w_sem.at[2 + k]))
    for load in own_block:
        load.start()
    w_up = pltpu.make_async_copy(up_hbm.at[0], upv, w_sem.at[0])
    w_down = pltpu.make_async_copy(down_hbm.at[0], downv, w_sem.at[1])
    w_up.start()
    w_down.start()

    partners = [at_z(1), at_z(-1)] + [at_x(j) for j in range(1, nx)]
    if ny > 1:
        partners += [at_y(1), at_y(-1), other_core]
    barrier = pltpu.get_barrier_semaphore()
    for partner in partners:
        pl.semaphore_signal(barrier, inc=1, device_id=partner, device_id_type=MESH_ID)

    top = cfg.top
    gate = gate_ref[...]
    high = gate.astype(BF16).astype(F32)
    rest = gate - high
    middle = rest.astype(BF16).astype(F32)
    low = rest - middle
    stack = jnp.concatenate([ids_ref[...].astype(F32), high, middle, low], axis=0).astype(BF16)
    row_e = lax.broadcasted_iota(jnp.int32, (4 * top, 4 * top), 0)
    col_e = lax.broadcasted_iota(jnp.int32, (4 * top, 4 * top), 1)
    turned = mm(stack, jnp.where(row_e == col_e, 1.0, 0.0).astype(BF16), 0, 0)
    lane = lax.broadcasted_iota(jnp.int32, (tok, 128), 1)
    lane_e = (lane & (experts - 1)).astype(F32)
    hit = jnp.zeros((tok, 128), F32)
    split = jnp.zeros((tok, 128), F32)
    for k in range(top):
        match = turned[:, k:k + 1] == lane_e
        hit = hit + jnp.where(match, 1.0, 0.0)
        value = jnp.where(
            lane < 2 * experts, turned[:, top + k:top + k + 1],
            jnp.where(lane < 3 * experts, turned[:, 2 * top + k:2 * top + k + 1],
                      turned[:, 3 * top + k:3 * top + k + 1]))
        split = split + jnp.where(match, value, 0.0)
    row_t = lax.broadcasted_iota(jnp.int32, (tok, tok), 0)
    col_t = lax.broadcasted_iota(jnp.int32, (tok, tok), 1)
    earlier = jnp.where(col_t < row_t, 1.0, 0.0).astype(BF16)
    before = mm(earlier, hit.astype(BF16))
    place = jnp.where(hit > 0.5, before, -1.0)
    table = jnp.where(lane < experts, place, jnp.where(lane < 4 * experts, split, 0.0))
    zmeta[0:tok, :] = table.astype(BF16)

    pl.semaphore_wait(barrier, len(partners))

    def ways(k):
        plus = nz // 2 if k % 2 == 0 else (nz - 1) // 2
        return plus, nz - 1 - plus

    def z_copy(k, way, hop):
        source = hop - 1 if way == 0 else (nz - hop + 1) % nz
        target = hop if way == 0 else nz - hop
        buf = zmeta if k == 2 * nc else zbuf.at[k]
        return copy(
            buf.at[pl.ds(source * tok, tok)], buf.at[pl.ds(target * tok, tok)],
            z_ss.at[k, target - 1], z_rs.at[k, target - 1], at_z(1 if way == 0 else -1))

    def z_step(k, hop):
        for way in (0, 1):
            if 1 <= hop <= ways(k)[way]:
                z_copy(k, way, hop).wait_recv()
            if hop + 1 <= ways(k)[way]:
                z_copy(k, way, hop + 1).start()

    def build_tables():
        meta = zmeta[...].astype(F32)
        lanes = lax.broadcasted_iota(jnp.int32, (seen, 128), 1)
        row = lax.broadcasted_iota(jnp.int32, (seen, 1), 0)
        source = jnp.zeros((seen, 1), F32)
        for q in range(1, nz):
            source = source + jnp.where(row >= q * tok, 1.0, 0.0)
        wide = -(-rows // 128) * 128
        place_lane = lax.broadcasted_iota(jnp.int32, (seen, wide), 1)
        hot = jnp.zeros((seen, wide), F32)
        for j in range(nx):
            expert = z * nx + lax.rem(x + j, nx)
            spot = jnp.sum(jnp.where(lanes == expert, meta, 0.0), axis=1, keepdims=True)
            value = jnp.where(spot > -0.5, spot + cfg.slot * source + rx * j, -1.0).astype(jnp.int32)
            hot = hot + jnp.where(place_lane == value, 1.0, 0.0)
        onehot_t[...] = hot[:, 0:rows].astype(BF16)
        onehot[...] = hot.T[0:rows].astype(BF16)
        picked = mm(onehot[...], zmeta[...])
        lanes_r = lax.broadcasted_iota(jnp.int32, (rx, 128), 1)
        for j in range(nx):
            expert = z * nx + lax.rem(x + j, nx)
            mine = ((lanes_r & (experts - 1)) == expert) & (lanes_r >= experts)
            value = jnp.sum(jnp.where(mine, picked[j * rx:(j + 1) * rx], 0.0), axis=1, keepdims=True)
            gates[j * rx:(j + 1) * rx, :] = jnp.broadcast_to(value, (rx, 128))

    def x_copy(k, j):
        return copy(
            xsend.at[k, pl.ds((j - 1) * rx, rx)], xrecv.at[k, pl.ds(j * rx, rx)],
            x_ss.at[k, j - 1], x_rs.at[k, j - 1], at_x(j))

    def dispatch(k):
        packed = mm(onehot[...], zbuf[k])
        if k >= nc:
            packed = packed * gates[:, 0:1]
        packed = packed.astype(BF16)
        xsend[k] = packed[rx:]
        xrecv[k, 0:rx, :] = packed[0:rx]
        for j in range(1, nx):
            x_copy(k, j).start()

    def arrive(k):
        for j in range(1, nx):
            x_copy(k, j).wait_recv()
        if k < nc:
            if k == 0:
                w_up.wait()
            part = mm(xrecv[k], upv[k * cw:(k + 1) * cw, :])
            if k == 0:
                pre[...] = part
            else:
                pre[...] += part
        else:
            c = k - nc
            if c == 0:
                w_down.wait()
            part = mm(xrecv[k], downv[:, c * cw:(c + 1) * cw], 1, 1)
            if c == 0:
                lin[...] = part
            else:
                lin[...] += part
            at = c % (nc // 2) * cw
            g_down[c // (nc // 2), :, at:at + cw] = mm(hid[...], xrecv[k], 0, 0).astype(BF16)

    blk = 16

    def make_hidden():
        def body(i, carry):
            at = pl.ds(pl.multiple_of(i * blk, blk), blk)
            p = pre[at, :]
            hid[at, :] = (p * jax.nn.sigmoid(p)).astype(BF16)
            return carry
        lax.fori_loop(0, rows // blk, body, 0)

    def make_pre_grad():
        def body(i, carry):
            at = pl.ds(pl.multiple_of(i * blk, blk), blk)
            p = pre[at, :]
            s = jax.nn.sigmoid(p)
            pgr[at, :] = (lin[at, :] * (s * (1.0 + p * (1.0 - s)))).astype(BF16)
            return carry
        lax.fori_loop(0, rows // blk, body, 0)

    def c_copy(m, j):
        return copy(
            csend.at[m, pl.ds((j - 1) * rx, rx)], crecv.at[m, pl.ds(j * rx, rx)],
            c_ss.at[m, j - 1], c_rs.at[m, j - 1], at_x(-j))

    def send_back(m):
        c = m % nc
        if m < nc:
            out = mm(hid[...], downv[:, c * cw:(c + 1) * cw])
        else:
            out = mm(pgr[...], upv[c * cw:(c + 1) * cw, :], 1, 1)
        out = out.astype(BF16)
        csend[m] = out[rx:]
        crecv[m, 0:rx, :] = out[0:rx]
        for j in range(1, nx):
            c_copy(m, j).start()

    def s_copy(m, way, hop):
        plus, minus = ways(m)
        slot = plus - hop + 1 if way == 0 else nz - (minus - hop + 1)
        at = hop - 1 if way == 0 else plus + hop - 1
        return copy(
            pbuf.at[m, pl.ds(slot * tok, tok)], rsbuf.at[m, at],
            s_ss.at[m, at], s_rs.at[m, at], at_z(-1 if way == 0 else 1))

    def s_step(m, hop):
        for way in (0, 1):
            count = ways(m)[way]
            if 1 <= hop <= count:
                s_copy(m, way, hop).wait_recv()
                at = hop - 1 if way == 0 else ways(m)[0] + hop - 1
                got = rsbuf[m, at].astype(F32)
                left = count - hop
                if left == 0:
                    fin[m] += got
                else:
                    slot = left if way == 0 else nz - left
                    sl = slice(slot * tok, (slot + 1) * tok)
                    pbuf[m, sl, :] = (pbuf[m, sl, :].astype(F32) + got).astype(BF16)
            if hop + 1 <= count:
                s_copy(m, way, hop + 1).start()
        if hop == max(ways(m)):
            c = m % nc
            target = mixed_ref if m < nc else gtok_ref
            target[:, c * cw:(c + 1) * cw] = fin[m].astype(BF16)

    def combine(m):
        for j in range(1, nx):
            c_copy(m, j).wait_recv()
        got = crecv[m]
        if m < nc:
            got = (got.astype(F32) * gates[:, 0:1]).astype(BF16)
        part = mm(onehot_t[...], got)
        fin[m] = part[0:tok]
        pbuf[m, tok:, :] = part[tok:].astype(BF16)
        s_step(m, 0)

    pieces = [
        (g_down.at[0], c_down.at[0], r_down.at[0], f_down.at[0]),
        (g_down.at[1], c_down.at[1], r_down.at[1], f_down.at[1]),
        (g_up.at[0], c_up.at[0], r_up.at[0], f_up.at[0]),
        (g_up.at[1], c_up.at[1], r_up.at[1], f_up.at[1]),
    ]

    def y_sizes(w):
        half = pieces[w][0].shape[0] // 2
        return half, half // 4, half // 8

    def y_copies(w):
        g, cr, r, f = pieces[w]
        half, shard, part = y_sizes(w)

        def of(step, b=0):
            return pl.multiple_of(lax.rem(y + step + ny, ny) * shard + b * part, part)

        def final(step, b, count):
            first = core * half + of(step, b)
            if w < 2:
                return gdown_ref.at[0, pl.ds(pl.multiple_of(first, part), count), pl.ds(w * (width // 2), width // 2)]
            return gup_ref.at[0, pl.ds(pl.multiple_of((w - 2) * (width // 2) + first, part), count)]

        def sem(i):
            return y_ss.at[w, i], y_rs.at[w, i]

        return dict(
            core=lambda: copy(g.at[pl.ds(pl.multiple_of((1 - core) * half, half), half)], cr, *sem(0), other_core),
            far_a=lambda: copy(cr.at[pl.ds(of(2, 0), part)], r.at[0], *sem(1), at_y(1)),
            far_b=lambda: copy(cr.at[pl.ds(of(2, 1), part)], r.at[1], *sem(2), at_y(-1)),
            near_b=lambda: copy(cr.at[pl.ds(of(1, 1), part)], r.at[2], *sem(3), at_y(1)),
            near_a=lambda: copy(cr.at[pl.ds(of(-1, 0), part)], r.at[3], *sem(4), at_y(-1)),
            two_a=lambda: copy(r.at[0], r.at[4], *sem(5), at_y(1)),
            two_b=lambda: copy(r.at[1], r.at[5], *sem(6), at_y(-1)),
            out_p=lambda: copy(f, final(0, 0, shard), *sem(7), at_y(1)),
            out_m=lambda: copy(f, final(0, 0, shard), *sem(8), at_y(-1)),
            out_c=lambda: copy(f, final(0, 0, shard), *sem(9), other_core),
            fwd_a=lambda: copy(final(-1, 0, part), final(-1, 0, part), *sem(10), at_y(1)),
            fwd_b=lambda: copy(final(1, 1, part), final(1, 1, part), *sem(11), at_y(-1)),
            cor_p=lambda: copy(final(-1, 0, shard), final(-1, 0, shard), *sem(12), other_core),
            cor_m=lambda: copy(final(1, 0, shard), final(1, 0, shard), *sem(13), other_core),
            cor_f=lambda: copy(final(2, 0, shard), final(2, 0, shard), *sem(14), other_core),
            own=lambda: pltpu.make_async_copy(f, final(0, 0, shard), l_sem.at[w]),
        )

    def add_rows(target, t0, source, s0, count, extra=None):
        size = 16 if count % 16 == 0 else count

        def body(i, carry):
            a = pl.ds(pl.multiple_of(t0 + i * size, size), size)
            b = pl.ds(pl.multiple_of(s0 + i * size, size), size)
            target[a, :] = (target[a, :].astype(F32) + source[b, :].astype(F32)).astype(BF16)
            return carry
        lax.fori_loop(0, count // size, body, 0)

    def y_step(w, step):
        g, cr, r, f = pieces[w]
        half, shard, part = y_sizes(w)
        cp = y_copies(w)

        def of(move, b=0):
            return pl.multiple_of(lax.rem(y + move + ny, ny) * shard + b * part, part)

        if step == 1:
            cp["core"]().start()
        elif step == 2:
            cp["core"]().wait_recv()
            add_rows(cr, 0, g, pl.multiple_of(core * half, half), half)
            for name in ("far_a", "far_b", "near_b", "near_a"):
                cp[name]().start()
        elif step == 3:
            cp["far_a"]().wait_recv()
            add_rows(r.at[0], 0, cr, of(1, 0), part)
            cp["two_a"]().start()
            cp["far_b"]().wait_recv()
            add_rows(r.at[1], 0, cr, of(-1, 1), part)
            cp["two_b"]().start()
        elif step == 4:
            for name in ("near_a", "near_b", "two_a", "two_b"):
                cp[name]().wait_recv()
            size = 16 if part % 16 == 0 else part
            for b, near, two in ((0, 3, 4), (1, 2, 5)):
                def body(i, carry):
                    a = pl.ds(pl.multiple_of(i * size, size), size)
                    c = pl.ds(pl.multiple_of(of(0, b) + i * size, size), size)
                    total = cr[c, :].astype(F32) + r[near, a, :].astype(F32) + r[two, a, :].astype(F32)
                    f[pl.ds(pl.multiple_of(b * part + i * size, size), size), :] = total.astype(BF16)
                    return carry
                lax.fori_loop(0, part // size, body, 0)
            for name in ("out_p", "out_m", "out_c", "own"):
                cp[name]().start()
        elif step == 5:
            cp["out_p"]().wait_recv()
            cp["fwd_a"]().start()
            cp["cor_p"]().start()
            cp["out_m"]().wait_recv()
            cp["fwd_b"]().start()
            cp["cor_m"]().start()
        elif step == 6:
            cp["fwd_a"]().wait_recv()
            cp["fwd_b"]().wait_recv()
            cp["cor_f"]().start()
        elif step == 7:
            for name in ("out_c", "cor_p", "cor_m", "cor_f"):
                cp[name]().wait_recv()
            cp["own"]().wait()

    hops = nz // 2
    do_y = ny > 1
    per = nc // 2

    def y_run(*steps):
        if do_y:
            for w, step in steps:
                y_step(w, step)

    def weight_grad_up(p):
        for c in range(p * per, (p + 1) * per):
            at = (c - p * per) * cw
            g_up[p, at:at + cw, :] = mm(xrecv[c], pgr[...], 0, 0).astype(BF16)

    def arrived(k):
        arrive(k)
        if k == nc - 1:
            make_hidden()
        if k == nc + per - 1:
            y_run((0, 1))

    events = []
    for h in range(hops + 1):
        events.append((h - 0.5, 2 * nc, h))
    for k in range(2 * nc):
        for h in range(hops + 1):
            events.append((h if k == 0 else k + h + 1, k, h))
    events.sort()
    for _, k, h in events:
        if h == 0 and k < 2 * nc:
            own_block[k].wait()
        z_step(k, h)
        if h == hops:
            if k == 2 * nc:
                build_tables()
            else:
                dispatch(k)
                if k >= LAG:
                    arrived(k - LAG)
    back = 0
    for k in range(2 * nc - LAG, 2 * nc):
        if k >= 2 * nc - 2:
            send_back(back)
            back += 1
        arrived(k)
    y_run((1, 1), (0, 2))
    send_back(back)
    back += 1
    make_pre_grad()
    weight_grad_up(0)
    y_run((2, 1), (0, 3))
    send_back(back)
    back += 1
    weight_grad_up(1)
    y_run((3, 1), (1, 2))
    plan = [
        [(0, 4), (2, 2)],
        [(1, 3), (3, 2)],
        [(0, 5), (1, 4)],
        [(2, 3), (0, 6)],
        [(1, 5), (2, 4), (3, 3)],
        [(1, 6), (2, 5), (3, 4)],
        [(2, 6), (3, 5), (0, 7)],
        [(3, 6), (1, 7)],
        [],
        [(2, 7)],
        [],
        [(3, 7)],
    ]
    count = 2 * nc
    for m in range(count + hops):
        if back < count:
            send_back(back)
            back += 1
        if m < count:
            combine(m)
        for h in range(hops, 0, -1):
            if 0 <= m - h < count:
                s_step(m - h, h)
        if m < len(plan):
            y_run(*plan[m])
    y_run(*[step for late in plan[count + hops:] for step in late])

    for k in range(2 * nc + 1):
        for way in (0, 1):
            for h in range(1, ways(k)[way] + 1):
                z_copy(k, way, h).wait_send()
    for k in range(2 * nc):
        for j in range(1, nx):
            x_copy(k, j).wait_send()
            c_copy(k, j).wait_send()
        for way in (0, 1):
            for h in range(1, ways(k)[way] + 1):
                s_copy(k, way, h).wait_send()
    if do_y:
        for w in range(4):
            for name, cp in y_copies(w).items():
                if name != "own":
                    cp().wait_send()


def hand_out(results):
    anywhere = pl.BlockSpec(memory_space=pl.ANY)
    count = len(results)
    parts = 4

    def body(*refs):
        held, sems = refs[2 * count:3 * count], refs[3 * count]
        moves = []
        for i in range(count):
            pieces = parts if len(results[i].shape) == 3 else 1
            size = results[i].shape[-2] // pieces
            for p in range(pieces):
                at = (pl.ds(p * size, size),)
                if len(results[i].shape) == 3:
                    at = (0,) + at
                moves.append((
                    pltpu.make_async_copy(refs[i].at[at], held[i].at[at], sems.at[0, i, p]),
                    pltpu.make_async_copy(held[i].at[at], refs[count + i].at[at], sems.at[1, i, p])))
        for load, _ in moves:
            load.start()
        for load, store in moves:
            load.wait()
            store.start()
        for _, store in moves:
            store.wait()

    return pl.pallas_call(
        body,
        out_shape=tuple(jax.ShapeDtypeStruct(r.shape, r.dtype) for r in results),
        in_specs=[anywhere] * count,
        out_specs=(anywhere,) * count,
        scratch_shapes=[pltpu.VMEM(r.shape, r.dtype) for r in results] + [pltpu.SemaphoreType.DMA((2, count, parts))],
        compiler_params=pltpu.CompilerParams(vmem_limit_bytes=60 * 2**20),
        name="hand_out",
    )(*results)


def run(cfg, tokens, expert_ids, gate_weights, up_weight, down_weight, out_grad):
    tok, width, hid_w, nc, cw = cfg.tok, cfg.width, cfg.hidden, cfg.nc, cfg.cw
    rows, rx, seen, nz, nx = cfg.rows, cfg.rows_x, cfg.seen, cfg.nz, cfg.nx
    vmem = pl.BlockSpec(memory_space=pltpu.VMEM)
    anywhere = pl.BlockSpec(memory_space=pl.ANY)
    dma = pltpu.SemaphoreType.DMA
    scratch = [
        pltpu.VMEM((2 * nc, seen, cw), BF16),
        pltpu.VMEM((seen, 128), BF16),
        pltpu.VMEM((2 * nc, rows - rx, cw), BF16),
        pltpu.VMEM((2 * nc, rows, cw), BF16),
        pltpu.VMEM((width, hid_w), BF16),
        pltpu.VMEM((hid_w, width), BF16),
        pltpu.VMEM((rows, hid_w), F32),
        pltpu.VMEM((rows, hid_w), F32),
        pltpu.VMEM((rows, hid_w), BF16),
        pltpu.VMEM((rows, hid_w), BF16),
        pltpu.VMEM((rows, seen), BF16),
        pltpu.VMEM((seen, rows), BF16),
        pltpu.VMEM((rows, 128), F32),
        pltpu.VMEM((2 * nc, rows - rx, cw), BF16),
        pltpu.VMEM((2 * nc, rows, cw), BF16),
        pltpu.VMEM((2 * nc, seen, cw), BF16),
        pltpu.VMEM((2 * nc, nz - 1, tok, cw), BF16),
        pltpu.VMEM((2 * nc, tok, cw), F32),
        pltpu.VMEM((2, hid_w, width // 2), BF16),
        pltpu.VMEM((2, width // 2, hid_w), BF16),
        pltpu.VMEM((2, hid_w // 2, width // 2), BF16),
        pltpu.VMEM((2, width // 4, hid_w), BF16),
        pltpu.VMEM((2, 6, hid_w // 16, width // 2), BF16),
        pltpu.VMEM((2, 6, width // 32, hid_w), BF16),
        pltpu.VMEM((2, hid_w // 8, width // 2), BF16),
        pltpu.VMEM((2, width // 16, hid_w), BF16),
        dma((2 + 2 * nc,)),
        dma((2 * nc + 1, nz - 1)),
        dma((2 * nc + 1, nz - 1)),
        dma((2 * nc, nx - 1)),
        dma((2 * nc, nx - 1)),
        dma((2 * nc, nx - 1)),
        dma((2 * nc, nx - 1)),
        dma((2 * nc, nz - 1)),
        dma((2 * nc, nz - 1)),
        dma((4, 15)),
        dma((4, 15)),
        dma((4,)),
    ]
    results = pl.pallas_call(
        functools.partial(kernel, cfg),
        out_shape=(
            jax.ShapeDtypeStruct((tok, width), BF16),
            jax.ShapeDtypeStruct((tok, width), BF16),
            jax.ShapeDtypeStruct((1, width, hid_w), BF16),
            jax.ShapeDtypeStruct((1, hid_w, width), BF16),
        ),
        in_specs=[anywhere, anywhere, vmem, vmem, anywhere, anywhere],
        out_specs=(vmem, vmem, anywhere, anywhere),
        scratch_shapes=scratch,
        compiler_params=pltpu.CompilerParams(
            collective_id=0, has_side_effects=True, vmem_limit_bytes=60 * 2**20
        ),
        name="expert_layer",
    )(tokens, out_grad, expert_ids.T, gate_weights.T, up_weight, down_weight)
    return hand_out(results)


def solution(mesh):
    dp, experts = mesh.shape["dp"], mesh.shape["expert"]

    def shards(tokens, expert_ids, gate_weights, up_weight, down_weight, out_grad):
        cfg = Cfg(8, experts // 8, dp // 2, tokens.shape[0], expert_ids.shape[1], tokens.shape[1],
                  up_weight.shape[2], 4)
        return run(cfg, tokens, expert_ids, gate_weights, up_weight, down_weight, out_grad)

    return jax.shard_map(
        shards,
        mesh=mesh,
        in_specs=(
            P(("dp", "expert"), None),
            P(("dp", "expert"), None),
            P(("dp", "expert"), None),
            P("expert", None, None),
            P("expert", None, None),
            P(("dp", "expert"), None),
        ),
        out_specs=(
            P(("dp", "expert"), None),
            P(("dp", "expert"), None),
            P("expert", None, None),
            P("expert", None, None),
        ),
        check_vma=False,
    )
```

```python
import functools

import jax
import jax.numpy as jnp
from jax import lax
from jax.experimental import pallas as pl
from jax.experimental.pallas import tpu as pltpu
from jax.sharding import PartitionSpec as P

BF16 = jnp.bfloat16
F32 = jnp.float32
MESH_ID = pl.DeviceIdType.MESH
LAG = 2
FIRST = 0.5
STRAIGHT = 1
AHEAD = 2


def mm(left, right, left_dim=1, right_dim=0):
    return lax.dot_general(
        left, right, (((left_dim,), (right_dim,)), ((), ())), preferred_element_type=F32
    )


class Cfg:
    def __init__(self, nz, nx, ny, tok, top, width, hidden, nc):
        self.nz, self.nx, self.ny = nz, nx, ny
        self.tok, self.top, self.width, self.hidden, self.nc = tok, top, width, hidden, nc
        self.experts = nz * nx
        self.slot = tok * top * 3 // (2 * self.experts)
        self.rows_x = nz * self.slot
        self.rows = nx * self.rows_x
        self.seen = nz * tok
        self.cw = width // nc


def kernel(cfg, *refs):
    nz, nx, ny, tok, nc, cw = cfg.nz, cfg.nx, cfg.ny, cfg.tok, cfg.nc, cfg.cw
    rx, rows, seen, experts = cfg.rows_x, cfg.rows, cfg.seen, cfg.experts
    width, hid_w = cfg.width, cfg.hidden
    (tok_ref, og_ref, ids_ref, gate_ref, up_hbm, down_hbm, mixed_ref, gtok_ref, gup_ref, gdown_ref) = refs[:10]
    (zbuf, zmeta, xsend, xrecv, upv, downv, pre, lin, hid, pgr, onehot, onehot_t, gates,
     csend, crecv, pbuf, rsbuf, fin, g_down, g_up, c_down, c_up, r_down, r_up, f_down, f_up,
     w_sem, z_ss, z_rs, x_ss, x_rs, c_ss, c_rs, s_ss, s_rs, y_ss, y_rs, l_sem) = refs[10:]

    dp = lax.axis_index("dp")
    ex = lax.axis_index("expert")
    y, core = dp // 2, lax.rem(dp, 2)
    z, x = ex // nx, lax.rem(ex, nx)

    def at_z(step):
        return (dp, lax.rem(z + step + nz, nz) * nx + x)

    def at_x(step):
        return (dp, z * nx + lax.rem(x + step + nx, nx))

    def at_y(step):
        return (lax.rem(y + step + ny, ny) * 2 + core, ex)

    other_core = (y * 2 + 1 - core, ex)

    def copy(src, dst, ss, rs, to):
        return pltpu.make_async_remote_copy(
            src_ref=src, dst_ref=dst, send_sem=ss, recv_sem=rs, device_id=to, device_id_type=MESH_ID
        )

    own_block = []
    for k in range(2 * nc):
        c = k % nc
        source = tok_ref if k < nc else og_ref
        own_block.append(pltpu.make_async_copy(
            source.at[:, pl.ds(c * cw, cw)], zbuf.at[k, pl.ds(0, tok)], w_sem.at[2 + k]))
    for load in own_block:
        load.start()
    w_up = pltpu.make_async_copy(up_hbm.at[0], upv, w_sem.at[0])
    w_down = pltpu.make_async_copy(down_hbm.at[0], downv, w_sem.at[1])
    w_up.start()
    w_down.start()

    partners = [at_z(d) for d in range(1, nz)] + [at_x(j) for j in range(1, nx)]
    if ny > 1:
        partners += [at_y(1), at_y(-1), other_core]
    barrier = pltpu.get_barrier_semaphore()
    for partner in partners:
        pl.semaphore_signal(barrier, inc=1, device_id=partner, device_id_type=MESH_ID)

    top = cfg.top
    gate = gate_ref[...]
    high = gate.astype(BF16).astype(F32)
    rest = gate - high
    middle = rest.astype(BF16).astype(F32)
    low = rest - middle
    stack = jnp.concatenate([ids_ref[...].astype(F32), high, middle, low], axis=0).astype(BF16)
    row_e = lax.broadcasted_iota(jnp.int32, (4 * top, 4 * top), 0)
    col_e = lax.broadcasted_iota(jnp.int32, (4 * top, 4 * top), 1)
    turned = mm(stack, jnp.where(row_e == col_e, 1.0, 0.0).astype(BF16), 0, 0)
    lane = lax.broadcasted_iota(jnp.int32, (tok, 128), 1)
    lane_e = (lane & (experts - 1)).astype(F32)
    hit = jnp.zeros((tok, 128), F32)
    split = jnp.zeros((tok, 128), F32)
    for k in range(top):
        match = turned[:, k:k + 1] == lane_e
        hit = hit + jnp.where(match, 1.0, 0.0)
        value = jnp.where(
            lane < 2 * experts, turned[:, top + k:top + k + 1],
            jnp.where(lane < 3 * experts, turned[:, 2 * top + k:2 * top + k + 1],
                      turned[:, 3 * top + k:3 * top + k + 1]))
        split = split + jnp.where(match, value, 0.0)
    row_t = lax.broadcasted_iota(jnp.int32, (tok, tok), 0)
    col_t = lax.broadcasted_iota(jnp.int32, (tok, tok), 1)
    earlier = jnp.where(col_t < row_t, 1.0, 0.0).astype(BF16)
    before = mm(earlier, hit.astype(BF16))
    place = jnp.where(hit > 0.5, before, -1.0)
    table = jnp.where(lane < experts, place, jnp.where(lane < 4 * experts, split, 0.0))
    zmeta[0:tok, :] = table.astype(BF16)

    pl.semaphore_wait(barrier, len(partners))

    def ways(k):
        plus = nz // 2 if k % 2 == 0 else (nz - 1) // 2
        return plus, nz - 1 - plus

    def z_copy(k, way, hop):
        source = hop - 1 if way == 0 else (nz - hop + 1) % nz
        target = hop if way == 0 else nz - hop
        return copy(
            zbuf.at[k, pl.ds(source * tok, tok)], zbuf.at[k, pl.ds(target * tok, tok)],
            z_ss.at[k, target - 1], z_rs.at[k, target - 1], at_z(1 if way == 0 else -1))

    hw = cw // 2
    direct = sorted(range(1, nz), key=lambda d: -min(d, nz - d))

    def z_direct(part, d):
        if part == 2:
            return copy(
                zmeta.at[pl.ds(0, tok)], zmeta.at[pl.ds(d * tok, tok)],
                z_ss.at[2 * nc + 1, d - 1], z_rs.at[2 * nc + 1, d - 1], at_z(d))
        row, cols = (0 if part == 0 else 2 * nc), pl.ds(part * hw, hw)
        return copy(
            zbuf.at[0, pl.ds(0, tok), cols], zbuf.at[0, pl.ds(d * tok, tok), cols],
            z_ss.at[row, d - 1], z_rs.at[row, d - 1], at_z(d))

    def z_step(k, hop):
        for way in (0, 1):
            if 1 <= hop <= ways(k)[way]:
                z_copy(k, way, hop).wait_recv()
            if hop + 1 <= ways(k)[way]:
                z_copy(k, way, hop + 1).start()

    def build_tables():
        meta = zmeta[...].astype(F32)
        lanes = lax.broadcasted_iota(jnp.int32, (seen, 128), 1)
        row = lax.broadcasted_iota(jnp.int32, (seen, 1), 0)
        source = jnp.zeros((seen, 1), F32)
        for q in range(1, nz):
            source = source + jnp.where(row >= q * tok, 1.0, 0.0)
        wide = -(-rows // 128) * 128
        place_lane = lax.broadcasted_iota(jnp.int32, (seen, wide), 1)
        hot = jnp.zeros((seen, wide), F32)
        for j in range(nx):
            expert = z * nx + lax.rem(x + j, nx)
            spot = jnp.sum(jnp.where(lanes == expert, meta, 0.0), axis=1, keepdims=True)
            value = jnp.where(spot > -0.5, spot + cfg.slot * source + rx * j, -1.0).astype(jnp.int32)
            hot = hot + jnp.where(place_lane == value, 1.0, 0.0)
        onehot_t[...] = hot[:, 0:rows].astype(BF16)
        onehot[...] = hot.T[0:rows].astype(BF16)

    def build_gates():
        picked = mm(onehot[...], zmeta[...])
        lanes_r = lax.broadcasted_iota(jnp.int32, (rx, 128), 1)
        for j in range(nx):
            expert = z * nx + lax.rem(x + j, nx)
            mine = ((lanes_r & (experts - 1)) == expert) & (lanes_r >= experts)
            value = jnp.sum(jnp.where(mine, picked[j * rx:(j + 1) * rx], 0.0), axis=1, keepdims=True)
            gates[j * rx:(j + 1) * rx, :] = jnp.broadcast_to(value, (rx, 128))

    def x_copy(k, j, part=None):
        row = 2 * nc if part == 1 else k
        cols = pl.ds(0, cw) if part is None else pl.ds(part * hw, hw)
        return copy(
            xsend.at[k, pl.ds((j - 1) * rx, rx), cols], xrecv.at[k, pl.ds(j * rx, rx), cols],
            x_ss.at[row, j - 1], x_rs.at[row, j - 1], at_x(j))

    def dispatch(k, part=None):
        cols = slice(0, cw) if part is None else slice(part * hw, (part + 1) * hw)
        packed = mm(onehot[...], zbuf[k, :, cols])
        if k >= nc:
            packed = packed * gates[:, 0:1]
        packed = packed.astype(BF16)
        xsend[k, :, cols] = packed[rx:]
        xrecv[k, 0:rx, cols] = packed[0:rx]
        for j in range(1, nx):
            x_copy(k, j, part).start()

    def arrive(k):
        for j in range(1, nx):
            for part in (0, 1) if k == 0 else (None,):
                x_copy(k, j, part).wait_recv()
        if k < nc:
            if k == 0:
                w_up.wait()
            part = mm(xrecv[k], upv[k * cw:(k + 1) * cw, :])
            if k == 0:
                pre[...] = part
            else:
                pre[...] += part
        else:
            c = k - nc
            if c == 0:
                w_down.wait()
            part = mm(xrecv[k], downv[:, c * cw:(c + 1) * cw], 1, 1)
            if c == 0:
                lin[...] = part
            else:
                lin[...] += part
            at = c % (nc // 2) * cw
            g_down[c // (nc // 2), :, at:at + cw] = mm(hid[...], xrecv[k], 0, 0).astype(BF16)

    blk = 48

    def make_hidden():
        def body(i, carry):
            at = pl.ds(pl.multiple_of(i * blk, blk), blk)
            p = pre[at, :]
            hid[at, :] = (p * jax.nn.sigmoid(p)).astype(BF16)
            return carry
        lax.fori_loop(0, rows // blk, body, 0)

    def make_pre_grad():
        def body(i, carry):
            at = pl.ds(pl.multiple_of(i * blk, blk), blk)
            p = pre[at, :]
            s = jax.nn.sigmoid(p)
            pgr[at, :] = (lin[at, :] * (s * (1.0 + p * (1.0 - s)))).astype(BF16)
            return carry
        lax.fori_loop(0, rows // blk, body, 0)

    last = 2 * nc - 1

    def c_copy(m, j, part=None):
        row = 2 * nc if part == 1 else m
        cols = pl.ds(0, cw) if part is None else pl.ds(part * hw, hw)
        return copy(
            csend.at[m, pl.ds((j - 1) * rx, rx), cols], crecv.at[m, pl.ds(j * rx, rx), cols],
            c_ss.at[row, j - 1], c_rs.at[row, j - 1], at_x(-j))

    def send_back(m):
        c = m % nc
        if m < nc:
            out = mm(hid[...], downv[:, c * cw:(c + 1) * cw])
        else:
            out = mm(pgr[...], upv[c * cw:(c + 1) * cw, :], 1, 1)
        out = out.astype(BF16)
        csend[m] = out[rx:]
        crecv[m, 0:rx, :] = out[0:rx]
        for part in (0, 1) if m == last else (None,):
            for j in range(1, nx):
                c_copy(m, j, part).start()

    def s_copy(m, way, hop):
        plus, minus = ways(m)
        slot = plus - hop + 1 if way == 0 else nz - (minus - hop + 1)
        at = hop - 1 if way == 0 else plus + hop - 1
        return copy(
            pbuf.at[m, pl.ds(slot * tok, tok)], rsbuf.at[m, at],
            s_ss.at[m, at], s_rs.at[m, at], at_z(-1 if way == 0 else 1))

    def s_step(m, hop):
        for way in (0, 1):
            count = ways(m)[way]
            if 1 <= hop <= count:
                s_copy(m, way, hop).wait_recv()
                at = hop - 1 if way == 0 else ways(m)[0] + hop - 1
                got = rsbuf[m, at].astype(F32)
                left = count - hop
                if left == 0:
                    fin[m] += got
                else:
                    slot = left if way == 0 else nz - left
                    sl = slice(slot * tok, (slot + 1) * tok)
                    pbuf[m, sl, :] = (pbuf[m, sl, :].astype(F32) + got).astype(BF16)
            if hop + 1 <= count:
                s_copy(m, way, hop + 1).start()
        if hop == max(ways(m)):
            c = m % nc
            target = mixed_ref if m < nc else gtok_ref
            target[:, c * cw:(c + 1) * cw] = fin[m].astype(BF16)

    def combine(m, part=None):
        cols = slice(0, cw) if part is None else slice(part * hw, (part + 1) * hw)
        for j in range(1, nx):
            c_copy(m, j, part).wait_recv()
        got = crecv[m, :, cols]
        if m < nc:
            got = (got.astype(F32) * gates[:, 0:1]).astype(BF16)
        total = mm(onehot_t[...], got)
        fin[m, :, cols] = total[0:tok]
        pbuf[m, tok:, cols] = total[tok:].astype(BF16)
        if m < ring:
            s_step(m, 0)
        else:
            for d in direct:
                s_direct(m, part, d).start()

    ring = 2 * nc - STRAIGHT

    def s_direct(m, part, d):
        row = 2 * nc if part == 1 else m
        cols = pl.ds(0, cw) if part is None else pl.ds(part * hw, hw)
        return copy(
            pbuf.at[m, pl.ds(d * tok, tok), cols], rsbuf.at[m, d - 1, slice(None), cols],
            s_ss.at[row, d - 1], s_rs.at[row, d - 1], at_z(-d))

    def finish(m, part=None):
        cols = slice(0, cw) if part is None else slice(part * hw, (part + 1) * hw)
        total = fin[m, :, cols]
        for d in range(1, nz):
            s_direct(m, part, d).wait_recv()
            total = total + rsbuf[m, d - 1, :, cols].astype(F32)
        at = m % nc * cw + cols.start
        gtok_ref[:, at:at + cols.stop - cols.start] = total.astype(BF16)

    pieces = [
        (g_down.at[0], c_down.at[0], r_down.at[0], f_down.at[0]),
        (g_down.at[1], c_down.at[1], r_down.at[1], f_down.at[1]),
        (g_up.at[0], c_up.at[0], r_up.at[0], f_up.at[0]),
        (g_up.at[1], c_up.at[1], r_up.at[1], f_up.at[1]),
    ]

    def y_sizes(w):
        half = pieces[w][0].shape[0] // 2
        return half, half // 4, half // 8

    def y_copies(w):
        g, cr, r, f = pieces[w]
        half, shard, part = y_sizes(w)

        def of(step, b=0):
            return pl.multiple_of(lax.rem(y + step + ny, ny) * shard + b * part, part)

        def final(step, b, count):
            first = core * half + of(step, b)
            if w < 2:
                return gdown_ref.at[0, pl.ds(pl.multiple_of(first, part), count), pl.ds(w * (width // 2), width // 2)]
            return gup_ref.at[0, pl.ds(pl.multiple_of((w - 2) * (width // 2) + first, part), count)]

        def sem(i):
            return y_ss.at[w, i], y_rs.at[w, i]

        return dict(
            core=lambda: copy(g.at[pl.ds(pl.multiple_of((1 - core) * half, half), half)], cr, *sem(0), other_core),
            far_a=lambda: copy(cr.at[pl.ds(of(2, 0), part)], r.at[0], *sem(1), at_y(1)),
            far_b=lambda: copy(cr.at[pl.ds(of(2, 1), part)], r.at[1], *sem(2), at_y(-1)),
            near_b=lambda: copy(cr.at[pl.ds(of(1, 1), part)], r.at[2], *sem(3), at_y(1)),
            near_a=lambda: copy(cr.at[pl.ds(of(-1, 0), part)], r.at[3], *sem(4), at_y(-1)),
            two_a=lambda: copy(r.at[0], r.at[4], *sem(5), at_y(1)),
            two_b=lambda: copy(r.at[1], r.at[5], *sem(6), at_y(-1)),
            out_p=lambda: copy(f, final(0, 0, shard), *sem(7), at_y(1)),
            out_m=lambda: copy(f, final(0, 0, shard), *sem(8), at_y(-1)),
            out_c=lambda: copy(f, final(0, 0, shard), *sem(9), other_core),
            fwd_a=lambda: copy(final(-1, 0, part), final(-1, 0, part), *sem(10), at_y(1)),
            fwd_b=lambda: copy(final(1, 1, part), final(1, 1, part), *sem(11), at_y(-1)),
            cor_p=lambda: copy(final(-1, 0, shard), final(-1, 0, shard), *sem(12), other_core),
            cor_m=lambda: copy(final(1, 0, shard), final(1, 0, shard), *sem(13), other_core),
            cor_f=lambda: copy(final(2, 0, shard), final(2, 0, shard), *sem(14), other_core),
            own=lambda: pltpu.make_async_copy(f, final(0, 0, shard), l_sem.at[w]),
        )

    def add_rows(target, t0, source, s0, count, extra=None):
        size = 64 if count % 64 == 0 else count

        def body(i, carry):
            a = pl.ds(pl.multiple_of(t0 + i * size, size), size)
            b = pl.ds(pl.multiple_of(s0 + i * size, size), size)
            target[a, :] = (target[a, :].astype(F32) + source[b, :].astype(F32)).astype(BF16)
            return carry
        lax.fori_loop(0, count // size, body, 0)

    def y_step(w, step):
        g, cr, r, f = pieces[w]
        half, shard, part = y_sizes(w)
        cp = y_copies(w)

        def of(move, b=0):
            return pl.multiple_of(lax.rem(y + move + ny, ny) * shard + b * part, part)

        if step == 1:
            cp["core"]().start()
        elif step == 2:
            cp["core"]().wait_recv()
            add_rows(cr, 0, g, pl.multiple_of(core * half, half), half)
            for name in ("far_a", "far_b", "near_b", "near_a"):
                cp[name]().start()
        elif step == 3:
            cp["far_a"]().wait_recv()
            add_rows(r.at[0], 0, cr, of(1, 0), part)
            cp["two_a"]().start()
            cp["far_b"]().wait_recv()
            add_rows(r.at[1], 0, cr, of(-1, 1), part)
            cp["two_b"]().start()
        elif step == 4:
            for name in ("near_a", "near_b", "two_a", "two_b"):
                cp[name]().wait_recv()
            size = 64 if part % 64 == 0 else part
            for b, near, two in ((0, 3, 4), (1, 2, 5)):
                def body(i, carry):
                    a = pl.ds(pl.multiple_of(i * size, size), size)
                    c = pl.ds(pl.multiple_of(of(0, b) + i * size, size), size)
                    total = cr[c, :].astype(F32) + r[near, a, :].astype(F32) + r[two, a, :].astype(F32)
                    f[pl.ds(pl.multiple_of(b * part + i * size, size), size), :] = total.astype(BF16)
                    return carry
                lax.fori_loop(0, part // size, body, 0)
            for name in ("out_p", "out_m", "out_c", "own"):
                cp[name]().start()
        elif step == 5:
            cp["out_p"]().wait_recv()
            cp["fwd_a"]().start()
            cp["cor_p"]().start()
            cp["out_m"]().wait_recv()
            cp["fwd_b"]().start()
            cp["cor_m"]().start()
        elif step == 6:
            cp["fwd_a"]().wait_recv()
            cp["fwd_b"]().wait_recv()
            cp["cor_f"]().start()
        elif step == 7:
            for name in ("out_c", "cor_p", "cor_m", "cor_f"):
                cp[name]().wait_recv()
            cp["own"]().wait()

    hops = nz // 2
    do_y = ny > 1
    per = nc // 2

    def y_run(*steps):
        if do_y:
            for w, step in steps:
                y_step(w, step)

    def weight_grad_up(p):
        for c in range(p * per, (p + 1) * per):
            at = (c - p * per) * cw
            g_up[p, at:at + cw, :] = mm(xrecv[c], pgr[...], 0, 0).astype(BF16)

    def arrived(k):
        arrive(k)
        if k == nc - 1:
            make_hidden()
        if k == nc + per - 1:
            y_run((0, 1))

    own_block[0].wait()
    for part in (2, 0, 1):
        for d in direct:
            z_direct(part, d).start()
    events = [(FIRST, -1, 0), (FIRST + 1, -1, 1)]
    for k in range(1, 2 * nc):
        for h in range(hops + 1):
            events.append((k - 1 + h, k, h))
    events.sort()
    for _, k, h in events:
        if k < 0:
            if h == 0:
                for d in direct:
                    z_direct(2, d).wait_recv()
                build_tables()
            for d in direct:
                z_direct(h, d).wait_recv()
            dispatch(0, h)
            if h == 1:
                build_gates()
            continue
        if h == 0:
            own_block[k].wait()
        z_step(k, h)
        if h == hops:
            dispatch(k)
            if k >= LAG:
                arrived(k - LAG)
    back = 0
    for k in range(2 * nc - LAG, 2 * nc):
        if k >= 2 * nc - 2:
            send_back(back)
            back += 1
        arrived(k)
    y_run((1, 1), (0, 2))
    send_back(back)
    back += 1
    make_pre_grad()
    weight_grad_up(0)
    y_run((2, 1), (0, 3))
    if AHEAD > 2:
        send_back(back)
        back += 1
    weight_grad_up(1)
    y_run((3, 1), (1, 2))
    plan = [
        [(0, 4)],
        [(1, 3), (2, 2)],
        [(0, 5), (3, 2)],
        [(1, 4), (2, 3)],
        [(0, 6), (3, 3), (1, 5)],
        [(2, 4), (1, 6), (3, 4)],
        [(2, 5), (0, 7)],
        [(3, 5), (2, 6)],
        [(1, 7), (3, 6)],
        [(2, 7), (3, 7)],
    ]

    def ring_steps(m):
        for h in range(hops, 0, -1):
            if 0 <= m - h < ring:
                s_step(m - h, h)

    for m in range(last):
        while back <= min(last, m + AHEAD):
            send_back(back)
            back += 1
        ring_steps(m)
        combine(m)
        y_run(*plan[m])
    while back <= last:
        send_back(back)
        back += 1
    ring_steps(last)
    combine(last, 0)
    ring_steps(last + 1)
    y_run(*plan[last])
    combine(last, 1)
    for m in range(last + 2, last + hops):
        ring_steps(m)
    y_run(*plan[last + 1])
    for m in range(ring, last):
        finish(m)
    finish(last, 0)
    finish(last, 1)
    y_run(*plan[last + 2])

    for part in range(3):
        for d in range(1, nz):
            z_direct(part, d).wait_send()
            if part < 2:
                s_direct(last, part, d).wait_send()
    for m in range(ring, last):
        for d in range(1, nz):
            s_direct(m, None, d).wait_send()
    for k in range(2 * nc):
        for j in range(1, nx):
            for part in (0, 1) if k == 0 else (None,):
                x_copy(k, j, part).wait_send()
            for part in (0, 1) if k == last else (None,):
                c_copy(k, j, part).wait_send()
        for way in (0, 1):
            for h in range(1, ways(k)[way] + 1):
                if k > 0:
                    z_copy(k, way, h).wait_send()
                if k < ring:
                    s_copy(k, way, h).wait_send()
    if do_y:
        for w in range(4):
            for name, cp in y_copies(w).items():
                if name != "own":
                    cp().wait_send()


def hand_out(results):
    anywhere = pl.BlockSpec(memory_space=pl.ANY)
    count = len(results)
    parts = 4

    def body(*refs):
        held, sems = refs[2 * count:3 * count], refs[3 * count]
        moves = []
        for i in range(count):
            pieces = parts if len(results[i].shape) == 3 else 1
            size = results[i].shape[-2] // pieces
            for p in range(pieces):
                at = (pl.ds(p * size, size),)
                if len(results[i].shape) == 3:
                    at = (0,) + at
                moves.append((
                    pltpu.make_async_copy(refs[i].at[at], held[i].at[at], sems.at[0, i, p]),
                    pltpu.make_async_copy(held[i].at[at], refs[count + i].at[at], sems.at[1, i, p])))
        for load, _ in moves:
            load.start()
        for load, store in moves:
            load.wait()
            store.start()
        for _, store in moves:
            store.wait()

    return pl.pallas_call(
        body,
        out_shape=tuple(jax.ShapeDtypeStruct(r.shape, r.dtype) for r in results),
        in_specs=[anywhere] * count,
        out_specs=(anywhere,) * count,
        scratch_shapes=[pltpu.VMEM(r.shape, r.dtype) for r in results] + [pltpu.SemaphoreType.DMA((2, count, parts))],
        compiler_params=pltpu.CompilerParams(vmem_limit_bytes=60 * 2**20),
        name="hand_out",
    )(*results)


def run(cfg, tokens, expert_ids, gate_weights, up_weight, down_weight, out_grad):
    tok, width, hid_w, nc, cw = cfg.tok, cfg.width, cfg.hidden, cfg.nc, cfg.cw
    rows, rx, seen, nz, nx = cfg.rows, cfg.rows_x, cfg.seen, cfg.nz, cfg.nx
    vmem = pl.BlockSpec(memory_space=pltpu.VMEM)
    anywhere = pl.BlockSpec(memory_space=pl.ANY)
    dma = pltpu.SemaphoreType.DMA
    scratch = [
        pltpu.VMEM((2 * nc, seen, cw), BF16),
        pltpu.VMEM((seen, 128), BF16),
        pltpu.VMEM((2 * nc, rows - rx, cw), BF16),
        pltpu.VMEM((2 * nc, rows, cw), BF16),
        pltpu.VMEM((width, hid_w), BF16),
        pltpu.VMEM((hid_w, width), BF16),
        pltpu.VMEM((rows, hid_w), F32),
        pltpu.VMEM((rows, hid_w), F32),
        pltpu.VMEM((rows, hid_w), BF16),
        pltpu.VMEM((rows, hid_w), BF16),
        pltpu.VMEM((rows, seen), BF16),
        pltpu.VMEM((seen, rows), BF16),
        pltpu.VMEM((rows, 128), F32),
        pltpu.VMEM((2 * nc, rows - rx, cw), BF16),
        pltpu.VMEM((2 * nc, rows, cw), BF16),
        pltpu.VMEM((2 * nc, seen, cw), BF16),
        pltpu.VMEM((2 * nc, nz - 1, tok, cw), BF16),
        pltpu.VMEM((2 * nc, tok, cw), F32),
        pltpu.VMEM((2, hid_w, width // 2), BF16),
        pltpu.VMEM((2, width // 2, hid_w), BF16),
        pltpu.VMEM((2, hid_w // 2, width // 2), BF16),
        pltpu.VMEM((2, width // 4, hid_w), BF16),
        pltpu.VMEM((2, 6, hid_w // 16, width // 2), BF16),
        pltpu.VMEM((2, 6, width // 32, hid_w), BF16),
        pltpu.VMEM((2, hid_w // 8, width // 2), BF16),
        pltpu.VMEM((2, width // 16, hid_w), BF16),
        dma((2 + 2 * nc,)),
        dma((2 * nc + 2, nz - 1)),
        dma((2 * nc + 2, nz - 1)),
        dma((2 * nc + 1, nx - 1)),
        dma((2 * nc + 1, nx - 1)),
        dma((2 * nc + 1, nx - 1)),
        dma((2 * nc + 1, nx - 1)),
        dma((2 * nc + 1, nz - 1)),
        dma((2 * nc + 1, nz - 1)),
        dma((4, 15)),
        dma((4, 15)),
        dma((4,)),
    ]
    results = pl.pallas_call(
        functools.partial(kernel, cfg),
        out_shape=(
            jax.ShapeDtypeStruct((tok, width), BF16),
            jax.ShapeDtypeStruct((tok, width), BF16),
            jax.ShapeDtypeStruct((1, width, hid_w), BF16),
            jax.ShapeDtypeStruct((1, hid_w, width), BF16),
        ),
        in_specs=[anywhere, anywhere, vmem, vmem, anywhere, anywhere],
        out_specs=(vmem, vmem, anywhere, anywhere),
        scratch_shapes=scratch,
        compiler_params=pltpu.CompilerParams(
            collective_id=0, has_side_effects=True, vmem_limit_bytes=60 * 2**20
        ),
        name="expert_layer",
    )(tokens, out_grad, expert_ids.T, gate_weights.T, up_weight, down_weight)
    return hand_out(results)


def solution(mesh):
    dp, experts = mesh.shape["dp"], mesh.shape["expert"]

    def shards(tokens, expert_ids, gate_weights, up_weight, down_weight, out_grad):
        cfg = Cfg(8, experts // 8, dp // 2, tokens.shape[0], expert_ids.shape[1], tokens.shape[1],
                  up_weight.shape[2], 4)
        return run(cfg, tokens, expert_ids, gate_weights, up_weight, down_weight, out_grad)

    return jax.shard_map(
        shards,
        mesh=mesh,
        in_specs=(
            P(("dp", "expert"), None),
            P(("dp", "expert"), None),
            P(("dp", "expert"), None),
            P("expert", None, None),
            P("expert", None, None),
            P(("dp", "expert"), None),
        ),
        out_specs=(
            P(("dp", "expert"), None),
            P(("dp", "expert"), None),
            P("expert", None, None),
            P("expert", None, None),
        ),
        check_vma=False,
    )
```

```python
import functools

import jax
import jax.numpy as jnp
from jax import lax
from jax.experimental import pallas as pl
from jax.experimental.pallas import tpu as pltpu
from jax.sharding import PartitionSpec as P

BF16 = jnp.bfloat16
F32 = jnp.float32
MESH_ID = pl.DeviceIdType.MESH
LAG = 2
FIRST = 0.5
STRAIGHT = 1
AHEAD = 2


def mm(left, right, left_dim=1, right_dim=0):
    return lax.dot_general(
        left, right, (((left_dim,), (right_dim,)), ((), ())), preferred_element_type=F32
    )


class Cfg:
    def __init__(self, nz, nx, ny, tok, top, width, hidden, nc):
        self.nz, self.nx, self.ny = nz, nx, ny
        self.tok, self.top, self.width, self.hidden, self.nc = tok, top, width, hidden, nc
        self.experts = nz * nx
        self.slot = tok * top * 3 // (2 * self.experts)
        self.rows_x = nz * self.slot
        self.rows = nx * self.rows_x
        self.seen = nz * tok
        self.cw = width // nc


def kernel(cfg, *refs):
    nz, nx, ny, tok, nc, cw = cfg.nz, cfg.nx, cfg.ny, cfg.tok, cfg.nc, cfg.cw
    rx, rows, seen, experts = cfg.rows_x, cfg.rows, cfg.seen, cfg.experts
    width, hid_w = cfg.width, cfg.hidden
    (tok_ref, og_ref, ids_ref, gate_ref, up_hbm, down_hbm, mixed_ref, gtok_ref, gup_ref, gdown_ref) = refs[:10]
    (zbuf, zmeta, xsend, xrecv, upv, downv, pre, lin, hid, pgr, onehot, onehot_t, gates,
     csend, crecv, pbuf, rsbuf, fin, g_down, g_up, c_down, c_up, r_down, r_up, f_down, f_up,
     w_sem, z_ss, z_rs, x_ss, x_rs, c_ss, c_rs, s_ss, s_rs, y_ss, y_rs, l_sem) = refs[10:]

    dp = lax.axis_index("dp")
    ex = lax.axis_index("expert")
    y, core = dp // 2, lax.rem(dp, 2)
    z, x = ex // nx, lax.rem(ex, nx)

    def at_z(step):
        return (dp, lax.rem(z + step + nz, nz) * nx + x)

    def at_x(step):
        return (dp, z * nx + lax.rem(x + step + nx, nx))

    def at_y(step):
        return (lax.rem(y + step + ny, ny) * 2 + core, ex)

    other_core = (y * 2 + 1 - core, ex)

    def copy(src, dst, ss, rs, to):
        return pltpu.make_async_remote_copy(
            src_ref=src, dst_ref=dst, send_sem=ss, recv_sem=rs, device_id=to, device_id_type=MESH_ID
        )

    own_block = []
    for k in range(2 * nc):
        c = k % nc
        source = tok_ref if k < nc else og_ref
        own_block.append(pltpu.make_async_copy(
            source.at[:, pl.ds(c * cw, cw)], zbuf.at[k, pl.ds(0, tok)], w_sem.at[2 + k]))
    for load in own_block:
        load.start()
    w_up = pltpu.make_async_copy(up_hbm.at[0], upv, w_sem.at[0])
    w_down = pltpu.make_async_copy(down_hbm.at[0], downv, w_sem.at[1])
    w_up.start()
    w_down.start()

    partners = [at_z(d) for d in range(1, nz)] + [at_x(j) for j in range(1, nx)]
    if ny > 1:
        partners += [at_y(1), at_y(-1), other_core]
    barrier = pltpu.get_barrier_semaphore()
    for partner in partners:
        pl.semaphore_signal(barrier, inc=1, device_id=partner, device_id_type=MESH_ID)

    top = cfg.top
    gate = gate_ref[...]
    high = gate.astype(BF16).astype(F32)
    rest = gate - high
    middle = rest.astype(BF16).astype(F32)
    low = rest - middle
    stack = jnp.concatenate([ids_ref[...].astype(F32), high, middle, low], axis=0).astype(BF16)
    row_e = lax.broadcasted_iota(jnp.int32, (4 * top, 4 * top), 0)
    col_e = lax.broadcasted_iota(jnp.int32, (4 * top, 4 * top), 1)
    turned = mm(stack, jnp.where(row_e == col_e, 1.0, 0.0).astype(BF16), 0, 0)
    lane = lax.broadcasted_iota(jnp.int32, (tok, 128), 1)
    lane_e = (lane & (experts - 1)).astype(F32)
    hit = jnp.zeros((tok, 128), F32)
    split = jnp.zeros((tok, 128), F32)
    for k in range(top):
        match = turned[:, k:k + 1] == lane_e
        hit = hit + jnp.where(match, 1.0, 0.0)
        value = jnp.where(
            lane < 2 * experts, turned[:, top + k:top + k + 1],
            jnp.where(lane < 3 * experts, turned[:, 2 * top + k:2 * top + k + 1],
                      turned[:, 3 * top + k:3 * top + k + 1]))
        split = split + jnp.where(match, value, 0.0)
    row_t = lax.broadcasted_iota(jnp.int32, (tok, tok), 0)
    col_t = lax.broadcasted_iota(jnp.int32, (tok, tok), 1)
    earlier = jnp.where(col_t < row_t, 1.0, 0.0).astype(BF16)
    before = mm(earlier, hit.astype(BF16))
    place = jnp.where(hit > 0.5, before, -1.0)
    table = jnp.where(lane < experts, place, jnp.where(lane < 4 * experts, split, 0.0))
    zmeta[0:tok, :] = table.astype(BF16)

    pl.semaphore_wait(barrier, len(partners))

    def ways(k):
        plus = nz // 2 if k % 2 == 0 else (nz - 1) // 2
        return plus, nz - 1 - plus

    def z_copy(k, way, hop):
        source = hop - 1 if way == 0 else (nz - hop + 1) % nz
        target = hop if way == 0 else nz - hop
        return copy(
            zbuf.at[k, pl.ds(source * tok, tok)], zbuf.at[k, pl.ds(target * tok, tok)],
            z_ss.at[k, target - 1], z_rs.at[k, target - 1], at_z(1 if way == 0 else -1))

    hw = cw // 2
    direct = sorted(range(1, nz), key=lambda d: -min(d, nz - d))

    def z_direct(part, d):
        if part == 2:
            return copy(
                zmeta.at[pl.ds(0, tok)], zmeta.at[pl.ds(d * tok, tok)],
                z_ss.at[2 * nc + 1, d - 1], z_rs.at[2 * nc + 1, d - 1], at_z(d))
        row, cols = (0 if part == 0 else 2 * nc), pl.ds(part * hw, hw)
        return copy(
            zbuf.at[0, pl.ds(0, tok), cols], zbuf.at[0, pl.ds(d * tok, tok), cols],
            z_ss.at[row, d - 1], z_rs.at[row, d - 1], at_z(d))

    def z_step(k, hop):
        for way in (0, 1):
            if 1 <= hop <= ways(k)[way]:
                z_copy(k, way, hop).wait_recv()
            if hop + 1 <= ways(k)[way]:
                z_copy(k, way, hop + 1).start()

    def build_tables():
        meta = zmeta[...].astype(F32)
        lanes = lax.broadcasted_iota(jnp.int32, (seen, 128), 1)
        row = lax.broadcasted_iota(jnp.int32, (seen, 1), 0)
        source = jnp.zeros((seen, 1), F32)
        for q in range(1, nz):
            source = source + jnp.where(row >= q * tok, 1.0, 0.0)
        wide = -(-rows // 128) * 128
        place_lane = lax.broadcasted_iota(jnp.int32, (seen, wide), 1)
        hot = jnp.zeros((seen, wide), F32)
        for j in range(nx):
            expert = z * nx + lax.rem(x + j, nx)
            spot = jnp.sum(jnp.where(lanes == expert, meta, 0.0), axis=1, keepdims=True)
            value = jnp.where(spot > -0.5, spot + cfg.slot * source + rx * j, -1.0).astype(jnp.int32)
            hot = hot + jnp.where(place_lane == value, 1.0, 0.0)
        onehot_t[...] = hot[:, 0:rows].astype(BF16)
        onehot[...] = hot.T[0:rows].astype(BF16)

    def build_gates():
        picked = mm(onehot[...], zmeta[...])
        lanes_r = lax.broadcasted_iota(jnp.int32, (rx, 128), 1)
        for j in range(nx):
            expert = z * nx + lax.rem(x + j, nx)
            mine = ((lanes_r & (experts - 1)) == expert) & (lanes_r >= experts)
            value = jnp.sum(jnp.where(mine, picked[j * rx:(j + 1) * rx], 0.0), axis=1, keepdims=True)
            gates[j * rx:(j + 1) * rx, :] = jnp.broadcast_to(value, (rx, 128))

    def x_copy(k, j, part=None):
        row = 2 * nc if part == 1 else k
        cols = pl.ds(0, cw) if part is None else pl.ds(part * hw, hw)
        return copy(
            xsend.at[k, pl.ds((j - 1) * rx, rx), cols], xrecv.at[k, pl.ds(j * rx, rx), cols],
            x_ss.at[row, j - 1], x_rs.at[row, j - 1], at_x(j))

    def dispatch(k, part=None):
        cols = slice(0, cw) if part is None else slice(part * hw, (part + 1) * hw)
        packed = mm(onehot[...], zbuf[k, :, cols])
        if k >= nc:
            packed = packed * gates[:, 0:1]
        packed = packed.astype(BF16)
        xsend[k, :, cols] = packed[rx:]
        xrecv[k, 0:rx, cols] = packed[0:rx]
        for j in range(1, nx):
            x_copy(k, j, part).start()

    def arrive(k):
        for j in range(1, nx):
            for part in (0, 1) if k == 0 else (None,):
                x_copy(k, j, part).wait_recv()
        if k < nc:
            if k == 0:
                w_up.wait()
            part = mm(xrecv[k], upv[k * cw:(k + 1) * cw, :])
            if k == 0:
                pre[...] = part
            else:
                pre[...] += part
        else:
            c = k - nc
            if c == 0:
                w_down.wait()
            part = mm(xrecv[k], downv[:, c * cw:(c + 1) * cw], 1, 1)
            if c == 0:
                lin[...] = part
            else:
                lin[...] += part
            at = c % (nc // 2) * cw
            g_down[c // (nc // 2), :, at:at + cw] = mm(hid[...], xrecv[k], 0, 0).astype(BF16)

    blk = 48

    def make_hidden():
        def body(i, carry):
            at = pl.ds(pl.multiple_of(i * blk, blk), blk)
            p = pre[at, :]
            hid[at, :] = (p * jax.nn.sigmoid(p)).astype(BF16)
            return carry
        lax.fori_loop(0, rows // blk, body, 0)

    def make_pre_grad():
        def body(i, carry):
            at = pl.ds(pl.multiple_of(i * blk, blk), blk)
            p = pre[at, :]
            s = jax.nn.sigmoid(p)
            pgr[at, :] = (lin[at, :] * (s * (1.0 + p * (1.0 - s)))).astype(BF16)
            return carry
        lax.fori_loop(0, rows // blk, body, 0)

    last = 2 * nc - 1

    def c_copy(m, j, part=None):
        row = 2 * nc if part == 1 else m
        cols = pl.ds(0, cw) if part is None else pl.ds(part * hw, hw)
        return copy(
            csend.at[m, pl.ds((j - 1) * rx, rx), cols], crecv.at[m, pl.ds(j * rx, rx), cols],
            c_ss.at[row, j - 1], c_rs.at[row, j - 1], at_x(-j))

    def send_back(m):
        c = m % nc
        if m < nc:
            out = mm(hid[...], downv[:, c * cw:(c + 1) * cw])
        else:
            out = mm(pgr[...], upv[c * cw:(c + 1) * cw, :], 1, 1)
        out = out.astype(BF16)
        csend[m] = out[rx:]
        crecv[m, 0:rx, :] = out[0:rx]
        for part in (0, 1) if m == last else (None,):
            for j in range(1, nx):
                c_copy(m, j, part).start()

    def s_copy(m, way, hop):
        plus, minus = ways(m)
        slot = plus - hop + 1 if way == 0 else nz - (minus - hop + 1)
        at = hop - 1 if way == 0 else plus + hop - 1
        return copy(
            pbuf.at[m, pl.ds(slot * tok, tok)], rsbuf.at[m, at],
            s_ss.at[m, at], s_rs.at[m, at], at_z(-1 if way == 0 else 1))

    def s_step(m, hop):
        for way in (0, 1):
            count = ways(m)[way]
            if 1 <= hop <= count:
                s_copy(m, way, hop).wait_recv()
                at = hop - 1 if way == 0 else ways(m)[0] + hop - 1
                got = rsbuf[m, at].astype(F32)
                left = count - hop
                if left == 0:
                    fin[m] += got
                else:
                    slot = left if way == 0 else nz - left
                    sl = slice(slot * tok, (slot + 1) * tok)
                    pbuf[m, sl, :] = (pbuf[m, sl, :].astype(F32) + got).astype(BF16)
            if hop + 1 <= count:
                s_copy(m, way, hop + 1).start()
        if hop == max(ways(m)):
            c = m % nc
            target = mixed_ref if m < nc else gtok_ref
            target[:, c * cw:(c + 1) * cw] = fin[m].astype(BF16)

    def combine(m, part=None):
        cols = slice(0, cw) if part is None else slice(part * hw, (part + 1) * hw)
        for j in range(1, nx):
            c_copy(m, j, part).wait_recv()
        got = crecv[m, :, cols]
        if m < nc:
            got = (got.astype(F32) * gates[:, 0:1]).astype(BF16)
        total = mm(onehot_t[...], got)
        fin[m, :, cols] = total[0:tok]
        pbuf[m, tok:, cols] = total[tok:].astype(BF16)
        if m < ring:
            s_step(m, 0)
        else:
            for d in direct:
                s_direct(m, part, d).start()

    ring = 2 * nc - STRAIGHT

    def s_direct(m, part, d):
        row = 2 * nc if part == 1 else m
        cols = pl.ds(0, cw) if part is None else pl.ds(part * hw, hw)
        return copy(
            pbuf.at[m, pl.ds(d * tok, tok), cols], rsbuf.at[m, d - 1, slice(None), cols],
            s_ss.at[row, d - 1], s_rs.at[row, d - 1], at_z(-d))

    def finish(m, part=None):
        cols = slice(0, cw) if part is None else slice(part * hw, (part + 1) * hw)
        total = fin[m, :, cols]
        for d in range(1, nz):
            s_direct(m, part, d).wait_recv()
            total = total + rsbuf[m, d - 1, :, cols].astype(F32)
        at = m % nc * cw + cols.start
        gtok_ref[:, at:at + cols.stop - cols.start] = total.astype(BF16)

    pieces = [
        (g_down.at[0], c_down.at[0], r_down.at[0], f_down.at[0]),
        (g_down.at[1], c_down.at[1], r_down.at[1], f_down.at[1]),
        (g_up.at[0], c_up.at[0], r_up.at[0], f_up.at[0]),
        (g_up.at[1], c_up.at[1], r_up.at[1], f_up.at[1]),
    ]

    def y_sizes(w):
        half = pieces[w][0].shape[0] // 2
        return half, half // 4, half // 8

    def y_copies(w):
        g, cr, r, f = pieces[w]
        half, shard, part = y_sizes(w)

        def of(step, b=0):
            return pl.multiple_of(lax.rem(y + step + ny, ny) * shard + b * part, part)

        def final(step, b, count):
            first = core * half + of(step, b)
            if w < 2:
                return gdown_ref.at[0, pl.ds(pl.multiple_of(first, part), count), pl.ds(w * (width // 2), width // 2)]
            return gup_ref.at[0, pl.ds(pl.multiple_of((w - 2) * (width // 2) + first, part), count)]

        def sem(i):
            return y_ss.at[w, i], y_rs.at[w, i]

        return dict(
            core=lambda: copy(g.at[pl.ds(pl.multiple_of((1 - core) * half, half), half)], cr, *sem(0), other_core),
            far_a=lambda: copy(cr.at[pl.ds(of(2, 0), part)], r.at[0], *sem(1), at_y(1)),
            far_b=lambda: copy(cr.at[pl.ds(of(2, 1), part)], r.at[1], *sem(2), at_y(-1)),
            near_b=lambda: copy(cr.at[pl.ds(of(1, 1), part)], r.at[2], *sem(3), at_y(1)),
            near_a=lambda: copy(cr.at[pl.ds(of(-1, 0), part)], r.at[3], *sem(4), at_y(-1)),
            two_a=lambda: copy(r.at[0], r.at[4], *sem(5), at_y(1)),
            two_b=lambda: copy(r.at[1], r.at[5], *sem(6), at_y(-1)),
            out_p=lambda: copy(f, final(0, 0, shard), *sem(7), at_y(1)),
            out_m=lambda: copy(f, final(0, 0, shard), *sem(8), at_y(-1)),
            out_c=lambda: copy(f, final(0, 0, shard), *sem(9), other_core),
            fwd_a=lambda: copy(final(-1, 0, part), final(-1, 0, part), *sem(10), at_y(1)),
            fwd_b=lambda: copy(final(1, 1, part), final(1, 1, part), *sem(11), at_y(-1)),
            cor_p=lambda: copy(final(-1, 0, shard), final(-1, 0, shard), *sem(12), other_core),
            cor_m=lambda: copy(final(1, 0, shard), final(1, 0, shard), *sem(13), other_core),
            cor_f=lambda: copy(final(2, 0, shard), final(2, 0, shard), *sem(14), other_core),
            own=lambda: pltpu.make_async_copy(f, final(0, 0, shard), l_sem.at[w]),
        )

    def add_rows(target, t0, source, s0, count, extra=None):
        size = 64 if count % 64 == 0 else count

        def body(i, carry):
            a = pl.ds(pl.multiple_of(t0 + i * size, size), size)
            b = pl.ds(pl.multiple_of(s0 + i * size, size), size)
            target[a, :] = (target[a, :].astype(F32) + source[b, :].astype(F32)).astype(BF16)
            return carry
        lax.fori_loop(0, count // size, body, 0)

    def y_step(w, step):
        g, cr, r, f = pieces[w]
        half, shard, part = y_sizes(w)
        cp = y_copies(w)

        def of(move, b=0):
            return pl.multiple_of(lax.rem(y + move + ny, ny) * shard + b * part, part)

        if step == 1:
            cp["core"]().start()
        elif step == 2:
            cp["core"]().wait_recv()
            add_rows(cr, 0, g, pl.multiple_of(core * half, half), half)
            for name in ("far_a", "far_b", "near_b", "near_a"):
                cp[name]().start()
        elif step == 3:
            cp["far_a"]().wait_recv()
            add_rows(r.at[0], 0, cr, of(1, 0), part)
            cp["two_a"]().start()
            cp["far_b"]().wait_recv()
            add_rows(r.at[1], 0, cr, of(-1, 1), part)
            cp["two_b"]().start()
        elif step == 4:
            for name in ("near_a", "near_b", "two_a", "two_b"):
                cp[name]().wait_recv()
            size = 64 if part % 64 == 0 else part
            for b, near, two in ((0, 3, 4), (1, 2, 5)):
                def body(i, carry):
                    a = pl.ds(pl.multiple_of(i * size, size), size)
                    c = pl.ds(pl.multiple_of(of(0, b) + i * size, size), size)
                    total = cr[c, :].astype(F32) + r[near, a, :].astype(F32) + r[two, a, :].astype(F32)
                    f[pl.ds(pl.multiple_of(b * part + i * size, size), size), :] = total.astype(BF16)
                    return carry
                lax.fori_loop(0, part // size, body, 0)
            for name in ("out_p", "out_m", "out_c", "own"):
                cp[name]().start()
        elif step == 5:
            cp["out_p"]().wait_recv()
            cp["fwd_a"]().start()
            cp["cor_p"]().start()
            cp["out_m"]().wait_recv()
            cp["fwd_b"]().start()
            cp["cor_m"]().start()
        elif step == 6:
            cp["fwd_a"]().wait_recv()
            cp["fwd_b"]().wait_recv()
            cp["cor_f"]().start()
        elif step == 7:
            for name in ("out_c", "cor_p", "cor_m", "cor_f"):
                cp[name]().wait_recv()
            cp["own"]().wait()

    hops = nz // 2
    do_y = ny > 1
    per = nc // 2

    def y_run(*steps):
        if do_y:
            for w, step in steps:
                y_step(w, step)

    def weight_grad_up(p):
        for c in range(p * per, (p + 1) * per):
            at = (c - p * per) * cw
            g_up[p, at:at + cw, :] = mm(xrecv[c], pgr[...], 0, 0).astype(BF16)

    def arrived(k):
        arrive(k)
        if k == nc - 1:
            make_hidden()
        if k == nc + per - 1:
            y_run((0, 1))

    own_block[0].wait()
    for part in (2, 0, 1):
        for d in direct:
            z_direct(part, d).start()
    events = [(FIRST, -1, 0), (FIRST + 1, -1, 1)]
    for k in range(1, 2 * nc):
        for h in range(hops + 1):
            events.append((k - 1 + h, k, h))
    events.sort()
    for _, k, h in events:
        if k < 0:
            if h == 0:
                for d in direct:
                    z_direct(2, d).wait_recv()
                build_tables()
            for d in direct:
                z_direct(h, d).wait_recv()
            dispatch(0, h)
            if h == 1:
                build_gates()
            continue
        if h == 0:
            own_block[k].wait()
        z_step(k, h)
        if h == hops:
            dispatch(k)
            if k >= LAG:
                arrived(k - LAG)
    back = 0
    for k in range(2 * nc - LAG, 2 * nc):
        if k >= 2 * nc - 2:
            send_back(back)
            back += 1
        arrived(k)
    y_run((1, 1), (0, 2))
    send_back(back)
    back += 1
    make_pre_grad()
    weight_grad_up(0)
    y_run((2, 1), (0, 3))
    if AHEAD > 2:
        send_back(back)
        back += 1
    weight_grad_up(1)
    y_run((3, 1), (1, 2))
    plan = [
        [],
        [(0, 4), (2, 2)],
        [(1, 3), (3, 2)],
        [(0, 5), (2, 3)],
        [(1, 4), (3, 3)],
        [(0, 6), (2, 4), (1, 5)],
        [(3, 4), (2, 5)],
        [(1, 6), (0, 7), (3, 5)],
        [(2, 6), (1, 7), (3, 6)],
        [(2, 7), (3, 7)],
    ]

    def ring_steps(m):
        for h in range(hops, 0, -1):
            if 0 <= m - h < ring:
                s_step(m - h, h)

    for m in range(last):
        while back <= min(last, m + AHEAD):
            send_back(back)
            back += 1
        ring_steps(m)
        combine(m)
        y_run(*plan[m])
    while back <= last:
        send_back(back)
        back += 1
    ring_steps(last)
    combine(last, 0)
    ring_steps(last + 1)
    y_run(*plan[last])
    combine(last, 1)
    for m in range(last + 2, last + hops):
        ring_steps(m)
    y_run(*plan[last + 1])
    for m in range(ring, last):
        finish(m)
    finish(last, 0)
    finish(last, 1)
    y_run(*plan[last + 2])

    for part in range(3):
        for d in range(1, nz):
            z_direct(part, d).wait_send()
            if part < 2:
                s_direct(last, part, d).wait_send()
    for m in range(ring, last):
        for d in range(1, nz):
            s_direct(m, None, d).wait_send()
    for k in range(2 * nc):
        for j in range(1, nx):
            for part in (0, 1) if k == 0 else (None,):
                x_copy(k, j, part).wait_send()
            for part in (0, 1) if k == last else (None,):
                c_copy(k, j, part).wait_send()
        for way in (0, 1):
            for h in range(1, ways(k)[way] + 1):
                if k > 0:
                    z_copy(k, way, h).wait_send()
                if k < ring:
                    s_copy(k, way, h).wait_send()
    if do_y:
        for w in range(4):
            for name, cp in y_copies(w).items():
                if name != "own":
                    cp().wait_send()


def hand_out(results):
    anywhere = pl.BlockSpec(memory_space=pl.ANY)
    count = len(results)
    parts = 4

    def body(*refs):
        held, sems = refs[2 * count:3 * count], refs[3 * count]
        moves = []
        for i in range(count):
            pieces = parts if len(results[i].shape) == 3 else 1
            size = results[i].shape[-2] // pieces
            for p in range(pieces):
                at = (pl.ds(p * size, size),)
                if len(results[i].shape) == 3:
                    at = (0,) + at
                moves.append((
                    pltpu.make_async_copy(refs[i].at[at], held[i].at[at], sems.at[0, i, p]),
                    pltpu.make_async_copy(held[i].at[at], refs[count + i].at[at], sems.at[1, i, p])))
        for load, _ in moves:
            load.start()
        for load, store in moves:
            load.wait()
            store.start()
        for _, store in moves:
            store.wait()

    return pl.pallas_call(
        body,
        out_shape=tuple(jax.ShapeDtypeStruct(r.shape, r.dtype) for r in results),
        in_specs=[anywhere] * count,
        out_specs=(anywhere,) * count,
        scratch_shapes=[pltpu.VMEM(r.shape, r.dtype) for r in results] + [pltpu.SemaphoreType.DMA((2, count, parts))],
        compiler_params=pltpu.CompilerParams(vmem_limit_bytes=60 * 2**20),
        name="hand_out",
    )(*results)


def run(cfg, tokens, expert_ids, gate_weights, up_weight, down_weight, out_grad):
    tok, width, hid_w, nc, cw = cfg.tok, cfg.width, cfg.hidden, cfg.nc, cfg.cw
    rows, rx, seen, nz, nx = cfg.rows, cfg.rows_x, cfg.seen, cfg.nz, cfg.nx
    vmem = pl.BlockSpec(memory_space=pltpu.VMEM)
    anywhere = pl.BlockSpec(memory_space=pl.ANY)
    dma = pltpu.SemaphoreType.DMA
    scratch = [
        pltpu.VMEM((2 * nc, seen, cw), BF16),
        pltpu.VMEM((seen, 128), BF16),
        pltpu.VMEM((2 * nc, rows - rx, cw), BF16),
        pltpu.VMEM((2 * nc, rows, cw), BF16),
        pltpu.VMEM((width, hid_w), BF16),
        pltpu.VMEM((hid_w, width), BF16),
        pltpu.VMEM((rows, hid_w), F32),
        pltpu.VMEM((rows, hid_w), F32),
        pltpu.VMEM((rows, hid_w), BF16),
        pltpu.VMEM((rows, hid_w), BF16),
        pltpu.VMEM((rows, seen), BF16),
        pltpu.VMEM((seen, rows), BF16),
        pltpu.VMEM((rows, 128), F32),
        pltpu.VMEM((2 * nc, rows - rx, cw), BF16),
        pltpu.VMEM((2 * nc, rows, cw), BF16),
        pltpu.VMEM((2 * nc, seen, cw), BF16),
        pltpu.VMEM((2 * nc, nz - 1, tok, cw), BF16),
        pltpu.VMEM((2 * nc, tok, cw), F32),
        pltpu.VMEM((2, hid_w, width // 2), BF16),
        pltpu.VMEM((2, width // 2, hid_w), BF16),
        pltpu.VMEM((2, hid_w // 2, width // 2), BF16),
        pltpu.VMEM((2, width // 4, hid_w), BF16),
        pltpu.VMEM((2, 6, hid_w // 16, width // 2), BF16),
        pltpu.VMEM((2, 6, width // 32, hid_w), BF16),
        pltpu.VMEM((2, hid_w // 8, width // 2), BF16),
        pltpu.VMEM((2, width // 16, hid_w), BF16),
        dma((2 + 2 * nc,)),
        dma((2 * nc + 2, nz - 1)),
        dma((2 * nc + 2, nz - 1)),
        dma((2 * nc + 1, nx - 1)),
        dma((2 * nc + 1, nx - 1)),
        dma((2 * nc + 1, nx - 1)),
        dma((2 * nc + 1, nx - 1)),
        dma((2 * nc + 1, nz - 1)),
        dma((2 * nc + 1, nz - 1)),
        dma((4, 15)),
        dma((4, 15)),
        dma((4,)),
    ]
    results = pl.pallas_call(
        functools.partial(kernel, cfg),
        out_shape=(
            jax.ShapeDtypeStruct((tok, width), BF16),
            jax.ShapeDtypeStruct((tok, width), BF16),
            jax.ShapeDtypeStruct((1, width, hid_w), BF16),
            jax.ShapeDtypeStruct((1, hid_w, width), BF16),
        ),
        in_specs=[anywhere, anywhere, vmem, vmem, anywhere, anywhere],
        out_specs=(vmem, vmem, anywhere, anywhere),
        scratch_shapes=scratch,
        compiler_params=pltpu.CompilerParams(
            collective_id=0, has_side_effects=True, vmem_limit_bytes=60 * 2**20
        ),
        name="expert_layer",
    )(tokens, out_grad, expert_ids.T, gate_weights.T, up_weight, down_weight)
    return hand_out(results)


def solution(mesh):
    dp, experts = mesh.shape["dp"], mesh.shape["expert"]

    def shards(tokens, expert_ids, gate_weights, up_weight, down_weight, out_grad):
        cfg = Cfg(8, experts // 8, dp // 2, tokens.shape[0], expert_ids.shape[1], tokens.shape[1],
                  up_weight.shape[2], 4)
        return run(cfg, tokens, expert_ids, gate_weights, up_weight, down_weight, out_grad)

    return jax.shard_map(
        shards,
        mesh=mesh,
        in_specs=(
            P(("dp", "expert"), None),
            P(("dp", "expert"), None),
            P(("dp", "expert"), None),
            P("expert", None, None),
            P("expert", None, None),
            P(("dp", "expert"), None),
        ),
        out_specs=(
            P(("dp", "expert"), None),
            P(("dp", "expert"), None),
            P("expert", None, None),
            P("expert", None, None),
        ),
        check_vma=False,
    )
```
